512 devices in a mesh: replica: 8 (over z_lo), fsdp: 64 (over y, x, z_hi, core).
Axes of the slice: x: 4, y: 4, z: 16 (z_hi: 2, z_lo: 8; z = z_hi * 8 + z_lo), core: 2. Of those that a mesh axis runs over, the one named last changes fastest.
Arguments:
- tokens: bfloat16 [131072, 7168], P(('replica', 'fsdp')), may hold values from -24 to 24
- cotangent: bfloat16 [131072, 128], P(('replica', 'fsdp')), may hold values from -0.046875 to 0.046875
- keep_mask: int32 [131072], P(('replica', 'fsdp')), may hold values 0 or 1
- key_weight: bfloat16 [8, 7168, 128], P('replica', 'fsdp'), may hold values from -0.0625 to 0.0625
- norm_gain: float32 [8, 7168], P('replica', 'fsdp'), may hold values from 0.1 to 1.9
- local_params: float32 [8, 8, 262144], P('replica', None, 'fsdp'), may hold values from -1400 to 1400
- global_params: float32 [8, 262144], P(None, 'fsdp'), may hold values from -4 to 4
- momentum: float32 [8, 262144], P(None, 'fsdp'), may hold values from -6 to 6
- fragment_order: int32 [8], replicated, may hold values from 0 to 7, each once
Outputs:
- weight_grad: float32 [8, 7168, 128], P('replica', 'fsdp')
- gain_grad: float32 [8, 7168], P('replica', 'fsdp')
- local_out: float32 [8, 8, 262144], P('replica', None, 'fsdp')
- global_out: float32 [8, 262144], P(None, 'fsdp')
- moment_out: float32 [8, 262144], P(None, 'fsdp')
The draws below stay inside these ranges and needn't reach their ends.
Inputs may be any that keep to these rules, and one draw needn't show every extreme that they name: `fragment_order`: its first 2 entries name the fragment's layers.
All inputs are finite; a program needn't handle non-finite values. No bound on the sum of `keep_mask` on one device may be relied on, other than what follows from the above.
Results may differ from the reference program's by a relative error of at most 0.005.
Values may be sent and summed in bfloat16 or wider, within the bound.
A program may use at most 64 MiB of HBM per device.

```python
import jax
import jax.numpy as jnp
from jax import lax

D = 7168
HD = 128
TOK_DEV = 256
P_DEV = 4096
HELD = 8
FRAG = 2
REPLICAS = 8
TOKENS = 131072
P_ALL = 262144
N_FSDP = 64


def common_base(key):
    return jax.random.truncated_normal(key, -4.0, 4.0, (HELD, P_ALL), jnp.float32)


def draw_global_params(key, part):
    base = common_base(key)
    return base


def draw_local_params(key, part):
    base = common_base(key)
    key = jax.random.fold_in(key, 2)
    key_row, key_col, key_own = jax.random.split(key, 3)
    row_scale = jnp.exp(jax.random.uniform(key_row, (1, HELD, 1), jnp.float32) * 2.302585)
    col_scale = jnp.exp(jax.random.uniform(key_col, (1, 1, P_ALL), jnp.float32) * 2.302585)
    shard = (jnp.arange(P_ALL) // P_DEV).astype(jnp.float32)
    ramp = 1.0 + 2.0 * shard / max(P_ALL // P_DEV - 1, 1)
    noise = jax.random.truncated_normal(key_own, -4.0, 4.0, (REPLICAS, HELD, P_ALL), jnp.float32)
    return base[None] + 0.3 * row_scale * col_scale * ramp[None, None, :] * noise


def place_ends(values, own_key, low, high):
    longest = values.shape.index(max(values.shape))
    spots = []
    for shift in (0, 1):
        where = [jax.random.randint(jax.random.fold_in(own_key, axis), (), 0, length) for axis, length in enumerate(values.shape)]
        where[longest] = (where[longest] + shift) % values.shape[longest]
        spots.append(tuple(where))
    return values.at[spots[0]].set(low).at[spots[1]].set(high)


def strengthened(drawn, stream_key, source, target, blocks, factor):
    def block_of(position):
        return (jnp.arange(drawn.shape[position]) // (drawn.shape[position] // blocks)).reshape((-1,) + (1,) * (drawn.ndim - 1 - position))

    first = jax.random.permutation(stream_key, blocks)[block_of(target)]
    other_side = (block_of(target) + blocks // 2) % blocks
    return jnp.where((block_of(source) == first) | (block_of(source) == other_side), factor * drawn, drawn)


def block_levels(stream_key, shape, cuts, low, largest):
    level, own = 1.0, jax.random.fold_in(stream_key, 6)
    for position, parts in cuts:
        steps = jnp.exp(jax.random.uniform(jax.random.fold_in(own, position), (parts,), jnp.float32, low / len(cuts), largest / len(cuts)))
        level = level * jnp.repeat(steps, shape[position] // parts).reshape([-1 if axis == position else 1 for axis in range(len(shape))])
    return level


def bell_draw(own_key, extent, deviation, bound, pieces=(), dtype=jnp.bfloat16):
    entries = jax.random.normal(own_key, extent, jnp.float32) * deviation
    if len(pieces) > 0:
        entries = block_levels(own_key, extent, pieces, -0.22, 0.18) * entries
    return jnp.clip(entries, min=-bound, max=bound).astype(dtype)


def noise_with(key, shape, scale, most, shards, heavy, kind=jnp.bfloat16):
    array = scale * jax.random.normal(key, shape, jnp.float32)
    if shards:
        array = array * block_levels(key, shape, shards, -0.22, 0.18)
    return jnp.clip(strengthened(array, jax.random.fold_in(key, 3), *heavy), -most, most).astype(kind)


def setup_inputs(seed: int = 0) -> dict:
    arg_keys = jax.random.split(jax.random.key(seed), 10)
    return {
        "tokens": noise_with(arg_keys[0], (TOKENS, D), 1.0, 24.0, ((0, 512),), (0, 1, 512, 6.0)),
        "cotangent": bell_draw(arg_keys[1], (TOKENS, HD), ((TOK_DEV * N_FSDP) ** -0.5), 0.046875, ((0, 512),)),
        "keep_mask": place_ends((jax.random.randint(arg_keys[2], (TOKENS,), 0, 4) < 3).astype(jnp.int32), jax.random.fold_in(arg_keys[2], 1), 0, 1),
        "key_weight": bell_draw(arg_keys[3], (REPLICAS, D, HD), D ** -0.5, 0.0625, ((0, 8), (1, 64))),
        "norm_gain": jnp.clip(1.0 + 0.18 * jax.random.normal(arg_keys[4], (REPLICAS, D), jnp.float32), 0.1, 1.9),
        "local_params": draw_local_params(jax.random.fold_in(arg_keys[9], 71), 0),
        "global_params": draw_global_params(jax.random.fold_in(arg_keys[9], 71), 0),
        "momentum": bell_draw(arg_keys[7], (HELD, P_ALL), 1.0, 6.0, ((1, 64),), jnp.float32),
        "fragment_order": jax.random.permutation(arg_keys[8], HELD).astype(jnp.int32),
    }


EPSILON = 1e-06
CLIP_RATE = 0.5
MOMENT = 0.9
OUTER_RATE = 0.7
MIX_RATE = 0.5

def group_grads(inputs):
    rows, cot_rows, mask_rows, weight, gain = inputs
    as_float = rows.astype(jnp.float32)
    inv_rms = lax.rsqrt(lax.optimization_barrier(jnp.mean(as_float * as_float, axis=1, keepdims=True)) + EPSILON)
    unit_rows = as_float * inv_rms
    normed = unit_rows.astype(jnp.bfloat16)
    masked = jnp.where(mask_rows[:, None] == 1, cot_rows, jnp.zeros_like(cot_rows))
    weight_grad = gain[:, None] * jnp.dot(normed.T, masked, preferred_element_type=jnp.float32)
    hidden_grad = jnp.dot(masked, weight.T, preferred_element_type=jnp.float32)
    gain_grad = lax.optimization_barrier(jnp.sum(hidden_grad * unit_rows, axis=0))
    return (weight_grad, gain_grad)

def reference(tokens, cotangent, keep_mask, key_weight, norm_gain, local_params, global_params, momentum, fragment_order):
    group = TOK_DEV * N_FSDP
    tok_groups = tokens.reshape(REPLICAS, group, D)
    cot_groups = cotangent.reshape(REPLICAS, group, HD)
    mask_groups = keep_mask.reshape(REPLICAS, group)
    weight_grad, gain_grad = lax.map(group_grads, (tok_groups, cot_groups, mask_groups, key_weight, norm_gain))
    frag_rows = fragment_order[:FRAG]
    local_rows = jnp.take(local_params, frag_rows, axis=1)
    glob_rows = jnp.take(global_params, frag_rows, axis=0)
    moment_rows = jnp.take(momentum, frag_rows, axis=0)
    delta = glob_rows[None] - local_rows
    averaged = lax.optimization_barrier(jnp.sum(delta, axis=0)) / REPLICAS
    squares = jnp.sum(averaged * averaged)
    limit = CLIP_RATE * jnp.sqrt(jnp.float32(FRAG * P_ALL))
    factor = jnp.minimum(1.0, limit / jnp.sqrt(squares + EPSILON))
    clipped = averaged * factor
    moment_new = MOMENT * moment_rows + clipped
    global_new = glob_rows - OUTER_RATE * (clipped + MOMENT * moment_new)
    merged = MIX_RATE * local_rows + (1.0 - MIX_RATE) * global_new[None]
    local_out = local_params.at[:, frag_rows].set(merged)
    global_out = global_params.at[frag_rows].set(global_new)
    moment_out = momentum.at[frag_rows].set(moment_new)
    return (weight_grad, gain_grad, local_out, global_out, moment_out)
```

```python
import functools

import jax
import jax.numpy as jnp
from jax import lax
from jax.experimental import pallas as pl
from jax.experimental.pallas import tpu as pltpu
from jax.sharding import PartitionSpec as P

FRAG = 2

EPSILON = 1e-06
CLIP_RATE = 0.5
MOMENT = 0.9
OUTER_RATE = 0.7
MIX_RATE = 0.5

NY, NX, NZ, NC = 4, 4, 2, 2
LANES = 128
TOKEN_BLOCK = 32
MESH = pl.DeviceIdType.MESH


def far_first(count):
    return sorted(range(count), key=lambda off: (-min(off, count - off), off))


def exchange_kernel(
    replicas,
    tok_hbm,
    cot_ref,
    mask_ref,
    loc_hbm,
    glob_hbm,
    order_ref,
    sum_ref,
    avg_ref,
    sq_ref,
    tok,
    loc,
    glob,
    masked,
    part,
    core_out,
    core_in,
    x1_out,
    x1_in,
    y1_out,
    y1_in,
    x2_out,
    x2_in,
    y2_out,
    y2_in,
    z_out,
    z_in,
    delta,
    delta_in,
    sq_out,
    sq_in,
    tok_sem,
    par_sem,
    core_sem,
    x1_sem,
    y1_sem,
    x2_sem,
    y2_sem,
    z_sem,
    rs_sem,
    ag_sem,
    sq_sem,
):
    rep = lax.axis_index("replica")
    me = lax.axis_index("fsdp")
    core = lax.rem(me, NC)
    z = lax.rem(me // NC, NZ)
    x = lax.rem(me // (NC * NZ), NX)
    y = me // (NC * NZ * NX)

    def device(yy, xx, zz, cc):
        return (rep, ((yy * NX + xx) * NZ + zz) * NC + cc)

    def x_peer(off):
        return device(y, lax.rem(x + off, NX), z, core)

    def y_peer(off):
        return device(lax.rem(y + off, NY), x, z, core)

    def rep_peer(off):
        return (lax.rem(rep + off, replicas), me)

    core_peer = device(y, x, z, 1 - core)
    z_peer = device(y, x, 1 - z, core)

    tokens, width = tok.shape
    rows = part.shape[0] // (NY * NX * NZ * NC)
    chunk = width // NY
    offs = far_first(NY)
    own = offs.index(0)

    token_copies = [
        pltpu.make_async_copy(
            tok_hbm.at[pl.ds(i * TOKEN_BLOCK, TOKEN_BLOCK)],
            tok.at[pl.ds(i * TOKEN_BLOCK, TOKEN_BLOCK)],
            tok_sem.at[i],
        )
        for i in range(tokens // TOKEN_BLOCK)
    ]
    for copy in token_copies:
        copy.start()
    loc_copy = pltpu.make_async_copy(loc_hbm.at[0], loc, par_sem.at[0])
    glob_copy = pltpu.make_async_copy(glob_hbm, glob, par_sem.at[1])
    loc_copy.start()
    glob_copy.start()

    barrier = pltpu.get_barrier_semaphore()
    peers = [core_peer, z_peer]
    peers += [x_peer(off) for off in range(1, NX)]
    peers += [y_peer(off) for off in range(1, NY)]
    peers += [rep_peer(off) for off in range(1, replicas)]
    for peer in peers:
        pl.semaphore_signal(barrier, inc=1, device_id=peer, device_id_type=MESH)

    cot_t = cot_ref[...].astype(jnp.float32).T
    keep = jnp.broadcast_to(mask_ref[...] == 1, cot_t.shape)
    masked[...] = jnp.where(keep, cot_t, 0.0).astype(jnp.bfloat16)

    for i, copy in enumerate(token_copies):
        copy.wait()
        for half in range(TOKEN_BLOCK // 16):
            at = pl.ds(i * TOKEN_BLOCK + half * 16, 16)
            sums = [jnp.zeros((16, LANES), jnp.float32) for _ in range(4)]
            for j in range(width // LANES):
                piece = tok[at, j * LANES : (j + 1) * LANES].astype(jnp.float32)
                sums[j % 4] += piece * piece
            total = jnp.sum((sums[0] + sums[1]) + (sums[2] + sums[3]), axis=1, keepdims=True)
            inv_rms = lax.rsqrt(total / width + EPSILON)
            for j in range(width // LANES):
                piece = tok[at, j * LANES : (j + 1) * LANES].astype(jnp.float32)
                tok[at, j * LANES : (j + 1) * LANES] = (piece * inv_rms).astype(jnp.bfloat16)

    loc_copy.wait()
    glob_copy.wait()
    per_row = loc.shape[1] // LANES
    for i in range(FRAG):
        layer = order_ref[i]
        diff = glob[pl.ds(layer, 1), :] - loc[pl.ds(layer, 1), :]
        for j in range(per_row):
            delta[i * per_row + j : i * per_row + j + 1, :] = diff[:, j * LANES : (j + 1) * LANES]

    pl.semaphore_wait(barrier, len(peers))

    sent = []

    def send(src, dst, sems, index, peer):
        copy = pltpu.make_async_remote_copy(
            src_ref=src,
            dst_ref=dst,
            send_sem=sems.at[0, index],
            recv_sem=sems.at[1, index],
            device_id=peer,
            device_id_type=MESH,
        )
        copy.start()
        sent.append(copy)
        return copy

    shard = delta.shape[0] // replicas
    rs = [
        send(
            delta.at[pl.ds(pl.multiple_of(lax.rem(rep + off, replicas) * shard, 8), shard)],
            delta_in.at[off - 1],
            rs_sem,
            off - 1,
            rep_peer(off),
        )
        for off in range(1, replicas)
    ]

    def outer_reduce():
        for copy in rs:
            copy.wait_recv()
        mine = pl.ds(pl.multiple_of(rep * shard, 8), shard)
        total = delta[mine, :]
        for off in range(1, replicas):
            total = total + delta_in[off - 1]
        avg_ref[mine, :] = total / replicas
        return [
            send(avg_ref.at[mine], avg_ref.at[mine], ag_sem, off - 1, rep_peer(off))
            for off in range(1, replicas)
        ]

    def square_round(at, base, value, targets):
        sq_out[at] = value
        return [
            send(sq_out.at[at], sq_in.at[base + i], sq_sem, base + i, peer)
            for i, peer in enumerate(targets)
        ]

    def square_sum(at, base, copies):
        total = sq_out[at]
        for i, copy in enumerate(copies):
            copy.wait_recv()
            total = total + sq_in[base + i]
        return total

    def column(off):
        return lax.rem(y + off, NY)

    def block_at(yy, xx, zz, cc):
        start = (((yy * NX + xx) * NZ + zz) * NC + cc) * rows
        return pl.ds(pl.multiple_of(start, 16), rows)

    def multiply(k):
        yy = column(offs[k])
        done = 0
        while done < chunk:
            size = min(256, chunk - done)
            at = pl.multiple_of(yy * chunk + done, LANES)
            product = jnp.dot(
                masked[...], tok[:, pl.ds(at, size)], preferred_element_type=jnp.float32
            )
            part[pl.ds(at, size), :] = product.T
            done += size
        for xx in range(NX):
            for zz in range(NZ):
                core_out[k, xx * NZ + zz] = part[block_at(yy, xx, zz, 1 - core), :].astype(
                    jnp.bfloat16
                )
        return send(core_out.at[k], core_in.at[k], core_sem, k, core_peer)

    def chip_sum(k, xx, zz):
        mine = part[block_at(column(offs[k]), xx, zz, core), :]
        return mine + core_in[k, xx * NZ + zz].astype(jnp.float32)

    x1, y1 = {}, {}

    def spread(k):
        core_copies[k].wait_recv()
        for off in far_first(NX)[:-1]:
            slot = k * (NX - 1) + off - 1
            x1_out[slot] = chip_sum(k, lax.rem(x + off, NX), 0).astype(jnp.bfloat16)
            x1[slot] = send(x1_out.at[slot], x1_in.at[slot], x1_sem, slot, x_peer(off))
        if k != own:
            slot = offs[k] - 1
            for xx in range(NX):
                y1_out[slot, xx] = chip_sum(k, xx, 1).astype(jnp.bfloat16)
            y1[slot] = send(y1_out.at[slot], y1_in.at[slot], y1_sem, slot, y_peer(offs[k]))

    def x_sum(k):
        total = chip_sum(k, x, 0)
        for off in range(1, NX):
            slot = k * (NX - 1) + off - 1
            x1[slot].wait_recv()
            total = total + x1_in[slot].astype(jnp.float32)
        return total

    def y_sum(xx):
        total = chip_sum(own, xx, 1)
        for off in range(1, NY):
            total = total + y1_in[off - 1, xx].astype(jnp.float32)
        return total

    x2, y2 = {}, {}

    def forward_x(k):
        slot = offs[k] - 1
        x2_out[slot] = x_sum(k).astype(jnp.bfloat16)
        x2[slot] = send(x2_out.at[slot], x2_in.at[slot], x2_sem, slot, y_peer(offs[k]))

    def forward_y():
        for off in range(1, NY):
            y1[off - 1].wait_recv()
        for off in far_first(NX)[:-1]:
            y2_out[off - 1] = y_sum(lax.rem(x + off, NX)).astype(jnp.bfloat16)
            y2[off - 1] = send(
                y2_out.at[off - 1], y2_in.at[off - 1], y2_sem, off - 1, x_peer(off)
            )

    core_copies = {}
    core_copies[0] = multiply(0)
    core_copies[1] = multiply(1)
    ag = outer_reduce()
    spread(0)
    y_squares = []

    def outer_gather():
        for copy in ag:
            copy.wait_recv()
        squared = avg_ref[...] * avg_ref[...]
        folded = squared[0:8]
        for i in range(1, squared.shape[0] // 8):
            folded = folded + squared[i * 8 : (i + 1) * 8]
        y_squares.extend(square_round(0, 0, folded, [y_peer(off) for off in range(1, NY)]))

    for k in range(2, NY):
        core_copies[k] = multiply(k)
        spread(k - 1)
        if k == 2:
            outer_gather()
    if not y_squares:
        outer_gather()
    x_squares = square_round(
        1, NY - 1, square_sum(0, 0, y_squares), [x_peer(off) for off in range(1, NX)]
    )
    spread(NY - 1)
    for k in range(NY - 1):
        forward_x(k)
    forward_y()
    base = NY + NX - 2
    core_squares = square_round(2, base, square_sum(1, NY - 1, x_squares), [core_peer])
    first = x_sum(own)
    for off in range(1, NY):
        x2[off - 1].wait_recv()
        first = first + x2_in[off - 1].astype(jnp.float32)
    second = y_sum(x)
    for off in range(1, NX):
        y2[off - 1].wait_recv()
        second = second + y2_in[off - 1].astype(jnp.float32)
    z_out[...] = jnp.where(z == 0, second, first).astype(jnp.bfloat16)
    z_copy = send(z_out, z_in, z_sem, 0, z_peer)
    sum_ref[...] = jnp.where(z == 0, first, second)
    z_squares = square_round(3, base + 1, square_sum(2, base, core_squares), [z_peer])
    sq_ref[...] = square_sum(3, base + 1, z_squares)
    z_copy.wait_recv()
    sum_ref[...] = sum_ref[...] + z_in[...].astype(jnp.float32)
    for copy in sent:
        copy.wait_send()


def exchange(tokens, cotangent, keep_mask, local_params, global_params, order, rows, replicas):
    count, width = tokens.shape
    heads = cotangent.shape[1]
    held, params = global_params.shape
    lines = FRAG * params // LANES
    squares = NY + NX
    vmem = pl.BlockSpec(memory_space=pltpu.VMEM)
    hbm = pl.BlockSpec(memory_space=pl.ANY)
    bf16, f32 = jnp.bfloat16, jnp.float32
    block = (rows, heads)
    return pl.pallas_call(
        functools.partial(exchange_kernel, replicas),
        out_shape=(
            jax.ShapeDtypeStruct(block, f32),
            jax.ShapeDtypeStruct((lines, LANES), f32),
            jax.ShapeDtypeStruct((8, LANES), f32),
        ),
        in_specs=[hbm, vmem, vmem, hbm, hbm, pl.BlockSpec(memory_space=pltpu.SMEM)],
        out_specs=(vmem, vmem, vmem),
        scratch_shapes=[
            pltpu.VMEM((count, width), bf16),
            pltpu.VMEM((held, params), f32),
            pltpu.VMEM((held, params), f32),
            pltpu.VMEM((heads, count), bf16),
            pltpu.VMEM((width, heads), f32),
            pltpu.VMEM((NY, NX * NZ) + block, bf16),
            pltpu.VMEM((NY, NX * NZ) + block, bf16),
            pltpu.VMEM((NY * (NX - 1),) + block, bf16),
            pltpu.VMEM((NY * (NX - 1),) + block, bf16),
            pltpu.VMEM((NY - 1, NX) + block, bf16),
            pltpu.VMEM((NY - 1, NX) + block, bf16),
            pltpu.VMEM((NY - 1,) + block, bf16),
            pltpu.VMEM((NY - 1,) + block, bf16),
            pltpu.VMEM((NX - 1,) + block, bf16),
            pltpu.VMEM((NX - 1,) + block, bf16),
            pltpu.VMEM(block, bf16),
            pltpu.VMEM(block, bf16),
            pltpu.VMEM((lines, LANES), f32),
            pltpu.VMEM((replicas - 1, lines // replicas, LANES), f32),
            pltpu.VMEM((4, 8, LANES), f32),
            pltpu.VMEM((squares, 8, LANES), f32),
            pltpu.SemaphoreType.DMA((count // TOKEN_BLOCK,)),
            pltpu.SemaphoreType.DMA((2,)),
            pltpu.SemaphoreType.DMA((2, NY)),
            pltpu.SemaphoreType.DMA((2, NY * (NX - 1))),
            pltpu.SemaphoreType.DMA((2, NY - 1)),
            pltpu.SemaphoreType.DMA((2, NY - 1)),
            pltpu.SemaphoreType.DMA((2, NX - 1)),
            pltpu.SemaphoreType.DMA((2, 1)),
            pltpu.SemaphoreType.DMA((2, replicas - 1)),
            pltpu.SemaphoreType.DMA((2, replicas - 1)),
            pltpu.SemaphoreType.DMA((2, squares)),
        ],
        compiler_params=pltpu.CompilerParams(
            collective_id=0, has_side_effects=True, vmem_limit_bytes=32 * 1024 * 1024
        ),
        cost_estimate=pl.CostEstimate(
            flops=2 * count * width * heads, bytes_accessed=2 * count * width, transcendentals=0
        ),
    )(tokens, cotangent, keep_mask.reshape(1, count), local_params, global_params, order)


def finish_kernel(
    count,
    order_ref,
    sum_ref,
    avg_ref,
    sq_ref,
    weight_ref,
    gain_ref,
    loc_ref,
    glob_ref,
    mom_ref,
    weight_out,
    gain_out,
    loc_out,
    glob_out,
    mom_out,
):
    total = sum_ref[...]
    rows, heads = total.shape
    scale = jnp.broadcast_to(gain_ref[...], (heads, rows)).T
    weight_out[0] = scale * total
    product = weight_ref[0].astype(jnp.float32) * total
    gain_out[...] = jnp.sum(product.T, axis=0, keepdims=True)

    squares = jnp.sum(sq_ref[...])
    limit = CLIP_RATE * jnp.sqrt(jnp.float32(count))
    factor = jnp.minimum(1.0, limit / jnp.sqrt(jnp.full((8, LANES), squares) + EPSILON))
    held, params = glob_ref.shape
    layer = lax.broadcasted_iota(jnp.int32, (held, LANES), 0)
    first = layer == order_ref[0]
    second = layer == order_ref[1]
    picked = first | second
    lines = params // LANES
    for j in range(lines):
        at = slice(j * LANES, (j + 1) * LANES)
        averaged = jnp.where(
            first,
            jnp.broadcast_to(avg_ref[j : j + 1, :], (held, LANES)),
            jnp.broadcast_to(avg_ref[lines + j : lines + j + 1, :], (held, LANES)),
        )
        loc, glob, mom = loc_ref[0, :, at], glob_ref[:, at], mom_ref[:, at]
        clipped = averaged * factor
        moment_new = MOMENT * mom + clipped
        global_new = glob - OUTER_RATE * (clipped + MOMENT * moment_new)
        merged = MIX_RATE * loc + (1.0 - MIX_RATE) * global_new
        loc_out[0, :, at] = jnp.where(picked, merged, loc)
        glob_out[:, at] = jnp.where(picked, global_new, glob)
        mom_out[:, at] = jnp.where(picked, moment_new, mom)


def finish(order, total, averaged, squares, weight, gain, local_params, global_params, momentum, count):
    vmem = pl.BlockSpec(memory_space=pltpu.VMEM)
    shapes = (
        jax.ShapeDtypeStruct(weight.shape, jnp.float32),
        jax.ShapeDtypeStruct(gain.shape, jnp.float32),
        jax.ShapeDtypeStruct(local_params.shape, jnp.float32),
        jax.ShapeDtypeStruct(global_params.shape, jnp.float32),
        jax.ShapeDtypeStruct(momentum.shape, jnp.float32),
    )
    return pl.pallas_call(
        functools.partial(finish_kernel, count),
        out_shape=shapes,
        in_specs=[pl.BlockSpec(memory_space=pltpu.SMEM)] + [vmem] * 8,
        out_specs=(vmem,) * 5,
        compiler_params=pltpu.CompilerParams(vmem_limit_bytes=16 * 1024 * 1024),
    )(order, total, averaged, squares, weight, gain, local_params, global_params, momentum)


def per_device(
    replicas,
    fsdp,
    tokens,
    cotangent,
    keep_mask,
    key_weight,
    norm_gain,
    local_params,
    global_params,
    momentum,
    fragment_order,
):
    total, averaged, squares = exchange(
        tokens,
        cotangent,
        keep_mask,
        local_params,
        global_params,
        fragment_order,
        key_weight.shape[1],
        replicas,
    )
    count = FRAG * global_params.shape[1] * fsdp
    return finish(
        fragment_order,
        total,
        averaged,
        squares,
        key_weight,
        norm_gain,
        local_params,
        global_params,
        momentum,
        count,
    )


def solution(mesh):
    in_specs = (
        P(("replica", "fsdp"), None),
        P(("replica", "fsdp"), None),
        P(("replica", "fsdp")),
        P("replica", "fsdp", None),
        P("replica", "fsdp"),
        P("replica", None, "fsdp"),
        P(None, "fsdp"),
        P(None, "fsdp"),
        P(),
    )
    out_specs = (
        P("replica", "fsdp", None),
        P("replica", "fsdp"),
        P("replica", None, "fsdp"),
        P(None, "fsdp"),
        P(None, "fsdp"),
    )
    return jax.shard_map(
        functools.partial(per_device, mesh.shape["replica"], mesh.shape["fsdp"]),
        mesh=mesh,
        in_specs=in_specs,
        out_specs=out_specs,
        check_vma=False,
    )
```

```python
import functools

import jax
import jax.numpy as jnp
from jax import lax
from jax.experimental import pallas as pl
from jax.experimental.pallas import tpu as pltpu
from jax.sharding import PartitionSpec as P

FRAG = 2

EPSILON = 1e-06
CLIP_RATE = 0.5
MOMENT = 0.9
OUTER_RATE = 0.7
MIX_RATE = 0.5

NY, NX, NZ, NC = 4, 4, 2, 2
LANES = 128
TOKEN_BLOCK = 32
MESH = pl.DeviceIdType.MESH


def far_first(count):
    return sorted(range(count), key=lambda off: (-min(off, count - off), off))


def exchange_kernel(
    replicas,
    tok_hbm,
    cot_hbm,
    mask_hbm,
    loc_hbm,
    glob_hbm,
    order_hbm,
    sum_ref,
    avg_ref,
    sq_ref,
    tok,
    cot,
    mask,
    loc,
    glob,
    order,
    masked,
    part,
    core_out,
    core_in,
    x1_out,
    x1_in,
    y1_out,
    y1_in,
    x2_out,
    x2_in,
    y2_out,
    y2_in,
    z_out,
    z_in,
    delta,
    delta_in,
    sq_out,
    sq_plane,
    sq_line,
    tok_sem,
    arg_sem,
    core_sem,
    x1_sem,
    y1_sem,
    x2_sem,
    y2_sem,
    z_sem,
    rs_sem,
    ag_sem,
    plane_sem,
    line_sem,
):
    rep = lax.axis_index("replica")
    me = lax.axis_index("fsdp")
    core = lax.rem(me, NC)
    z = lax.rem(me // NC, NZ)
    x = lax.rem(me // (NC * NZ), NX)
    y = me // (NC * NZ * NX)

    def device(yy, xx, zz, cc):
        return (rep, ((yy * NX + xx) * NZ + zz) * NC + cc)

    def plane_peer(dy, dx, dc=0):
        return device(lax.rem(y + dy, NY), lax.rem(x + dx, NX), z, lax.rem(core + dc, NC))

    def line_peer(dr, dz):
        return (lax.rem(rep + dr, replicas), device(y, x, lax.rem(z + dz, NZ), core)[1])

    core_peer = plane_peer(0, 0, 1)
    plane = [(dy, dx) for dy in far_first(NY) for dx in far_first(NX) if dy or dx]
    line = [(dr, dz) for dr in range(replicas) for dz in range(NZ) if dr or dz]

    tokens, width = tok.shape
    rows, heads = sum_ref.shape
    chunk = width // NY
    offs = far_first(NY)
    own = offs.index(0)
    x_rows = x1_out.shape[1]
    x_part, y_part = slice(0, x_rows), slice(x_rows, rows)

    arg_copies = [
        pltpu.make_async_copy(src, dst, arg_sem.at[i])
        for i, (src, dst) in enumerate(
            [(cot_hbm, cot), (mask_hbm, mask), (order_hbm, order), (loc_hbm.at[0], loc), (glob_hbm, glob)]
        )
    ]
    token_copies = [
        pltpu.make_async_copy(
            tok_hbm.at[pl.ds(i * TOKEN_BLOCK, TOKEN_BLOCK)],
            tok.at[pl.ds(i * TOKEN_BLOCK, TOKEN_BLOCK)],
            tok_sem.at[i],
        )
        for i in range(tokens // TOKEN_BLOCK)
    ]
    for copy in arg_copies + token_copies:
        copy.start()

    barrier = pltpu.get_barrier_semaphore()
    peers = [line_peer(dr, dz) for dr, dz in line]
    peers += [plane_peer(*offset) for offset in plane] + [core_peer]
    for peer in peers:
        pl.semaphore_signal(barrier, inc=1, device_id=peer, device_id_type=MESH)

    for copy in arg_copies:
        copy.wait()
    per_row = loc.shape[1] // LANES
    for i in range(FRAG):
        layer = order[i]
        diff = glob[pl.ds(layer, 1), :] - loc[pl.ds(layer, 1), :]
        for j in range(per_row):
            delta[i * per_row + j : i * per_row + j + 1, :] = diff[:, j * LANES : (j + 1) * LANES]

    cot_t = cot[...].astype(jnp.float32).T
    keep = jnp.broadcast_to(mask[...] == 1, cot_t.shape)
    masked[...] = jnp.where(keep, cot_t, 0.0).astype(jnp.bfloat16)

    for i, copy in enumerate(token_copies):
        copy.wait()
        for half in range(TOKEN_BLOCK // 16):
            at = pl.ds(i * TOKEN_BLOCK + half * 16, 16)
            sums = [jnp.zeros((16, LANES), jnp.float32) for _ in range(4)]
            for j in range(width // LANES):
                piece = tok[at, j * LANES : (j + 1) * LANES].astype(jnp.float32)
                sums[j % 4] += piece * piece
            total = jnp.sum((sums[0] + sums[1]) + (sums[2] + sums[3]), axis=1, keepdims=True)
            inv_rms = lax.rsqrt(total / width + EPSILON)
            for j in range(width // LANES):
                piece = tok[at, j * LANES : (j + 1) * LANES].astype(jnp.float32)
                tok[at, j * LANES : (j + 1) * LANES] = (piece * inv_rms).astype(jnp.bfloat16)

    pl.semaphore_wait(barrier, len(peers))

    sent = []

    def send(src, dst, sems, index, peer):
        copy = pltpu.make_async_remote_copy(
            src_ref=src,
            dst_ref=dst,
            send_sem=sems.at[0, index],
            recv_sem=sems.at[1, index],
            device_id=peer,
            device_id_type=MESH,
        )
        copy.start()
        sent.append(copy)
        return copy

    shard = delta.shape[0] // replicas
    rs = [
        send(
            delta.at[pl.ds(pl.multiple_of(lax.rem(rep + off, replicas) * shard, 8), shard)],
            delta_in.at[off - 1],
            rs_sem,
            off - 1,
            line_peer(off, 0),
        )
        for off in far_first(replicas)[:-1]
    ]

    def column(k):
        return lax.rem(y + offs[k], NY)

    def side(half):
        return 1 - z if half == 0 else z

    def block_at(yy, xx, zz, cc):
        start = (((yy * NX + xx) * NZ + zz) * NC + cc) * rows
        return pl.multiple_of(start, 16)

    core_copies = {}
    for half in range(2):
        for k in range(NY):
            if half == 0:
                done = 0
                while done < chunk:
                    size = min(256, chunk - done)
                    at = pl.multiple_of(column(k) * chunk + done, LANES)
                    product = jnp.dot(
                        masked[...], tok[:, pl.ds(at, size)], preferred_element_type=jnp.float32
                    )
                    part[pl.ds(at, size), :] = product.T
                    done += size
            slot = half * NY + k
            for xx in range(NX):
                at = block_at(column(k), xx, side(half), 1 - core)
                core_out[slot, xx] = part[pl.ds(at, rows), :].astype(jnp.bfloat16)
            core_copies[slot] = send(core_out.at[slot], core_in.at[slot], core_sem, slot, core_peer)

    def chip_sum(half, k, xx, at):
        start = block_at(column(k), xx, side(half), core) + at.start
        mine = part[pl.ds(start, at.stop - at.start), :]
        return mine + core_in[half * NY + k, xx, at].astype(jnp.float32)

    x1, y1, x2, y2 = {}, {}, {}, {}

    def x1_slot(half, k, off):
        return (half * NY + k) * (NX - 1) + off - 1

    def y_slot(half, off):
        return half * (NY - 1) + off - 1

    def x_slot(half, off):
        return half * (NX - 1) + off - 1

    def spread(half, k):
        core_copies[half * NY + k].wait_recv()
        for off in far_first(NX)[:-1]:
            slot = x1_slot(half, k, off)
            x1_out[slot] = chip_sum(half, k, lax.rem(x + off, NX), x_part).astype(jnp.bfloat16)
            x1[slot] = send(x1_out.at[slot], x1_in.at[slot], x1_sem, slot, plane_peer(0, off))
        if k != own:
            slot = y_slot(half, offs[k])
            for xx in range(NX):
                y1_out[slot, xx] = chip_sum(half, k, xx, y_part).astype(jnp.bfloat16)
            y1[slot] = send(
                y1_out.at[slot], y1_in.at[slot], y1_sem, slot, plane_peer(offs[k], 0)
            )

    def x_sum(half, k):
        total = chip_sum(half, k, x, x_part)
        for off in range(1, NX):
            slot = x1_slot(half, k, off)
            x1[slot].wait_recv()
            total = total + x1_in[slot].astype(jnp.float32)
        return total

    def y_sum(half, xx):
        total = chip_sum(half, own, xx, y_part)
        for off in range(1, NY):
            total = total + y1_in[y_slot(half, off), xx].astype(jnp.float32)
        return total

    def forward(half):
        for k in range(NY):
            if k != own:
                slot = y_slot(half, offs[k])
                x2_out[slot] = x_sum(half, k).astype(jnp.bfloat16)
                x2[slot] = send(
                    x2_out.at[slot], x2_in.at[slot], x2_sem, slot, plane_peer(offs[k], 0)
                )
        for off in range(1, NY):
            y1[y_slot(half, off)].wait_recv()
        for off in far_first(NX)[:-1]:
            slot = x_slot(half, off)
            y2_out[slot] = y_sum(half, lax.rem(x + off, NX)).astype(jnp.bfloat16)
            y2[slot] = send(y2_out.at[slot], y2_in.at[slot], y2_sem, slot, plane_peer(0, off))

    def gather(half):
        top = x_sum(half, own)
        low = y_sum(half, x)
        for off in range(1, NY):
            slot = y_slot(half, off)
            x2[slot].wait_recv()
            top = top + x2_in[slot].astype(jnp.float32)
        for off in range(1, NX):
            slot = x_slot(half, off)
            y2[slot].wait_recv()
            low = low + y2_in[slot].astype(jnp.float32)
        return top, low

    for k in range(NY):
        spread(0, k)

    for copy in rs:
        copy.wait_recv()
    mine = pl.ds(pl.multiple_of(rep * shard, 8), shard)
    total = delta[mine, :]
    for off in range(1, replicas):
        total = total + delta_in[off - 1]
    averaged = total / replicas
    avg_ref[mine, :] = averaged
    sq_out[0] = jnp.sum(averaged * averaged, axis=0, keepdims=True)
    pair_copy = send(sq_out.at[0], sq_plane.at[len(plane)], plane_sem, len(plane), core_peer)
    ag = [
        send(avg_ref.at[mine], avg_ref.at[mine], ag_sem, off - 1, line_peer(off, 0))
        for off in far_first(replicas)[:-1]
    ]
    pair_copy.wait_recv()
    sq_out[1] = sq_out[0] + sq_plane[len(plane)]
    plane_copies = [
        send(sq_out.at[1], sq_plane.at[i], plane_sem, i, plane_peer(*offset))
        for i, offset in enumerate(plane)
    ]
    for k in range(NY):
        spread(1, k)

    forward(0)

    squares = sq_out[1]
    for i, copy in enumerate(plane_copies):
        copy.wait_recv()
        squares = squares + sq_plane[i]
    sq_out[2] = squares
    place = rep * NZ + z
    sq_line[place] = squares
    line_copies = [
        send(sq_out.at[2], sq_line.at[place], line_sem, i, line_peer(dr, dz))
        for i, (dr, dz) in enumerate(line)
    ]

    top, low = gather(0)
    z_out[x_part] = top.astype(jnp.bfloat16)
    z_out[y_part] = low.astype(jnp.bfloat16)
    z_copy = send(z_out, z_in, z_sem, 0, line_peer(0, 1))

    forward(1)
    top, low = gather(1)
    for copy in ag:
        copy.wait_recv()
    for copy in line_copies:
        copy.wait_recv()
    squares = sq_line[0]
    for i in range(1, replicas * NZ):
        squares = squares + sq_line[i]
    sq_ref[...] = squares

    z_copy.wait_recv()
    sum_ref[x_part] = top + z_in[x_part].astype(jnp.float32)
    sum_ref[y_part] = low + z_in[y_part].astype(jnp.float32)
    for copy in sent:
        copy.wait_send()


def exchange(tokens, cotangent, keep_mask, local_params, global_params, order, rows, replicas):
    count, width = tokens.shape
    heads = cotangent.shape[1]
    held, params = global_params.shape
    lines = FRAG * params // LANES
    vmem = pl.BlockSpec(memory_space=pltpu.VMEM)
    hbm = pl.BlockSpec(memory_space=pltpu.HBM)
    bf16, f32 = jnp.bfloat16, jnp.float32
    x_rows = (rows // 16 + 1) // 2 * 16
    x_block, y_block = (x_rows, heads), (rows - x_rows, heads)
    peers = NY * NX - 1
    members = replicas * NZ
    return pl.pallas_call(
        functools.partial(exchange_kernel, replicas),
        out_shape=(
            jax.ShapeDtypeStruct((rows, heads), f32),
            jax.ShapeDtypeStruct((lines, LANES), f32),
            jax.ShapeDtypeStruct((1, LANES), f32),
        ),
        in_specs=[hbm] * 6,
        out_specs=(vmem, vmem, vmem),
        scratch_shapes=[
            pltpu.VMEM((count, width), bf16),
            pltpu.VMEM((count, heads), bf16),
            pltpu.VMEM((1, count), jnp.int32),
            pltpu.VMEM((held, params), f32),
            pltpu.VMEM((held, params), f32),
            pltpu.SMEM(order.shape, jnp.int32),
            pltpu.VMEM((heads, count), bf16),
            pltpu.VMEM((width, heads), f32),
            pltpu.VMEM((2 * NY, NX, rows, heads), bf16),
            pltpu.VMEM((2 * NY, NX, rows, heads), bf16),
            pltpu.VMEM((2 * NY * (NX - 1),) + x_block, bf16),
            pltpu.VMEM((2 * NY * (NX - 1),) + x_block, bf16),
            pltpu.VMEM((2 * (NY - 1), NX) + y_block, bf16),
            pltpu.VMEM((2 * (NY - 1), NX) + y_block, bf16),
            pltpu.VMEM((2 * (NY - 1),) + x_block, bf16),
            pltpu.VMEM((2 * (NY - 1),) + x_block, bf16),
            pltpu.VMEM((2 * (NX - 1),) + y_block, bf16),
            pltpu.VMEM((2 * (NX - 1),) + y_block, bf16),
            pltpu.VMEM((rows, heads), bf16),
            pltpu.VMEM((rows, heads), bf16),
            pltpu.VMEM((lines, LANES), f32),
            pltpu.VMEM((replicas - 1, lines // replicas, LANES), f32),
            pltpu.VMEM((3, 1, LANES), f32),
            pltpu.VMEM((peers + 1, 1, LANES), f32),
            pltpu.VMEM((members, 1, LANES), f32),
            pltpu.SemaphoreType.DMA((count // TOKEN_BLOCK,)),
            pltpu.SemaphoreType.DMA((5,)),
            pltpu.SemaphoreType.DMA((2, 2 * NY)),
            pltpu.SemaphoreType.DMA((2, 2 * NY * (NX - 1))),
            pltpu.SemaphoreType.DMA((2, 2 * (NY - 1))),
            pltpu.SemaphoreType.DMA((2, 2 * (NY - 1))),
            pltpu.SemaphoreType.DMA((2, 2 * (NX - 1))),
            pltpu.SemaphoreType.DMA((2, 1)),
            pltpu.SemaphoreType.DMA((2, replicas - 1)),
            pltpu.SemaphoreType.DMA((2, replicas - 1)),
            pltpu.SemaphoreType.DMA((2, peers + 1)),
            pltpu.SemaphoreType.DMA((2, members - 1)),
        ],
        compiler_params=pltpu.CompilerParams(
            collective_id=0, has_side_effects=True, vmem_limit_bytes=63 * 1024 * 1024
        ),
        cost_estimate=pl.CostEstimate(
            flops=2 * count * width * heads, bytes_accessed=2 * count * width, transcendentals=0
        ),
    )(tokens, cotangent, keep_mask.reshape(1, count), local_params, global_params, order)


def finish_kernel(
    count,
    order_hbm,
    sum_hbm,
    avg_hbm,
    sq_hbm,
    weight_hbm,
    gain_hbm,
    loc_hbm,
    glob_hbm,
    mom_hbm,
    weight_out,
    gain_out,
    loc_out,
    glob_out,
    mom_out,
    order,
    total,
    avg,
    sq,
    weight,
    gain,
    loc,
    glob,
    mom,
    weight_new,
    gain_new,
    loc_new,
    glob_new,
    mom_new,
    in_sem,
    out_sem,
):
    pairs = [
        (avg_hbm, avg),
        (sq_hbm, sq),
        (loc_hbm.at[0], loc),
        (glob_hbm, glob),
        (mom_hbm, mom),
        (order_hbm, order),
        (sum_hbm, total),
        (weight_hbm.at[0], weight),
        (gain_hbm, gain),
    ]
    loads = [pltpu.make_async_copy(src, dst, in_sem.at[i]) for i, (src, dst) in enumerate(pairs)]
    for copy in loads:
        copy.start()
    for copy in loads:
        copy.wait()

    squares = jnp.sum(sq[...])
    limit = CLIP_RATE * jnp.sqrt(jnp.float32(count))
    factor = jnp.minimum(1.0, limit / jnp.sqrt(jnp.full((8, LANES), squares) + EPSILON))
    held, params = glob.shape
    layer = lax.broadcasted_iota(jnp.int32, (held, LANES), 0)
    first = layer == order[0]
    second = layer == order[1]
    picked = first | second
    lines = params // LANES
    stores = []

    def store(src, dst, index):
        copy = pltpu.make_async_copy(src, dst, out_sem.at[index])
        copy.start()
        stores.append(copy)

    parts = 2
    for part in range(parts):
        for j in range(part * lines // parts, (part + 1) * lines // parts):
            at = slice(j * LANES, (j + 1) * LANES)
            averaged = jnp.where(
                first,
                jnp.broadcast_to(avg[j : j + 1, :], (held, LANES)),
                jnp.broadcast_to(avg[lines + j : lines + j + 1, :], (held, LANES)),
            )
            old_loc, old_glob, old_mom = loc[:, at], glob[:, at], mom[:, at]
            clipped = averaged * factor
            moment_new = MOMENT * old_mom + clipped
            global_new = old_glob - OUTER_RATE * (clipped + MOMENT * moment_new)
            merged = MIX_RATE * old_loc + (1.0 - MIX_RATE) * global_new
            loc_new[:, at] = jnp.where(picked, merged, old_loc)
            glob_new[:, at] = jnp.where(picked, global_new, old_glob)
            mom_new[:, at] = jnp.where(picked, moment_new, old_mom)
        span = pl.ds(part * params // parts, params // parts)
        store(loc_new.at[:, span], loc_out.at[0, :, span], 3 * part)
        store(glob_new.at[:, span], glob_out.at[:, span], 3 * part + 1)
        store(mom_new.at[:, span], mom_out.at[:, span], 3 * part + 2)

    summed = total[...]
    rows, heads = summed.shape
    scale = jnp.broadcast_to(gain[...], (heads, rows)).T
    weight_new[...] = scale * summed
    store(weight_new, weight_out.at[0], 3 * parts)
    product = weight[...].astype(jnp.float32) * summed
    gain_new[...] = jnp.sum(product.T, axis=0, keepdims=True)
    store(gain_new, gain_out, 3 * parts + 1)
    for copy in stores:
        copy.wait()


def finish(order, total, averaged, squares, weight, gain, local_params, global_params, momentum, count):
    hbm = pl.BlockSpec(memory_space=pltpu.HBM)
    f32 = jnp.float32
    shapes = (
        jax.ShapeDtypeStruct(weight.shape, f32),
        jax.ShapeDtypeStruct(gain.shape, f32),
        jax.ShapeDtypeStruct(local_params.shape, f32),
        jax.ShapeDtypeStruct(global_params.shape, f32),
        jax.ShapeDtypeStruct(momentum.shape, f32),
    )
    state = pltpu.VMEM(global_params.shape, f32)
    return pl.pallas_call(
        functools.partial(finish_kernel, count),
        out_shape=shapes,
        in_specs=[hbm] * 9,
        out_specs=(hbm,) * 5,
        scratch_shapes=[
            pltpu.SMEM(order.shape, jnp.int32),
            pltpu.VMEM(total.shape, f32),
            pltpu.VMEM(averaged.shape, f32),
            pltpu.VMEM(squares.shape, f32),
            pltpu.VMEM(weight.shape[1:], weight.dtype),
            pltpu.VMEM(gain.shape, f32),
            state,
            state,
            state,
            pltpu.VMEM(weight.shape[1:], f32),
            pltpu.VMEM(gain.shape, f32),
            state,
            state,
            state,
            pltpu.SemaphoreType.DMA((9,)),
            pltpu.SemaphoreType.DMA((8,)),
        ],
        compiler_params=pltpu.CompilerParams(vmem_limit_bytes=63 * 1024 * 1024),
    )(order, total, averaged, squares, weight, gain, local_params, global_params, momentum)


def per_device(
    replicas,
    fsdp,
    tokens,
    cotangent,
    keep_mask,
    key_weight,
    norm_gain,
    local_params,
    global_params,
    momentum,
    fragment_order,
):
    total, averaged, squares = exchange(
        tokens,
        cotangent,
        keep_mask,
        local_params,
        global_params,
        fragment_order,
        key_weight.shape[1],
        replicas,
    )
    count = FRAG * global_params.shape[1] * fsdp
    return finish(
        fragment_order,
        total,
        averaged,
        squares,
        key_weight,
        norm_gain,
        local_params,
        global_params,
        momentum,
        count,
    )


def solution(mesh):
    in_specs = (
        P(("replica", "fsdp"), None),
        P(("replica", "fsdp"), None),
        P(("replica", "fsdp")),
        P("replica", "fsdp", None),
        P("replica", "fsdp"),
        P("replica", None, "fsdp"),
        P(None, "fsdp"),
        P(None, "fsdp"),
        P(),
    )
    out_specs = (
        P("replica", "fsdp", None),
        P("replica", "fsdp"),
        P("replica", None, "fsdp"),
        P(None, "fsdp"),
        P(None, "fsdp"),
    )
    return jax.shard_map(
        functools.partial(per_device, mesh.shape["replica"], mesh.shape["fsdp"]),
        mesh=mesh,
        in_specs=in_specs,
        out_specs=out_specs,
        check_vma=False,
    )
```

```python
import functools

import jax
import jax.numpy as jnp
from jax import lax
from jax.experimental import pallas as pl
from jax.experimental.pallas import tpu as pltpu
from jax.sharding import PartitionSpec as P

FRAG = 2

EPSILON = 1e-06
CLIP_RATE = 0.5
MOMENT = 0.9
OUTER_RATE = 0.7
MIX_RATE = 0.5

NY, NX, NZ, NC = 4, 4, 2, 2
LANES = 128
TOKEN_BLOCK = 32
OWNERS = 4
MESH = pl.DeviceIdType.MESH


def far_first(count):
    return sorted(range(count), key=lambda off: (-min(off, count - off), off))


def exchange_kernel(
    replicas,
    tok_hbm,
    cot_hbm,
    mask_hbm,
    loc_hbm,
    glob_hbm,
    order_hbm,
    sum_ref,
    avg_ref,
    sq_ref,
    tok,
    cot,
    mask,
    loc,
    glob,
    order,
    masked,
    part,
    core_out,
    core_in,
    x1_out,
    x1_in,
    y1_out,
    y1_in,
    x2_out,
    x2_in,
    y2_out,
    y2_in,
    z_out,
    z_in,
    delta,
    delta_in,
    sq_out,
    sq_plane,
    sq_line,
    tok_sem,
    arg_sem,
    core_sem,
    x1_sem,
    y1_sem,
    x2_sem,
    y2_sem,
    z_sem,
    rs_sem,
    ag_sem,
    plane_sem,
    line_sem,
):
    rep = lax.axis_index("replica")
    me = lax.axis_index("fsdp")
    core = lax.rem(me, NC)
    z = lax.rem(me // NC, NZ)
    x = lax.rem(me // (NC * NZ), NX)
    y = me // (NC * NZ * NX)

    def device(yy, xx, zz, cc):
        return (rep, ((yy * NX + xx) * NZ + zz) * NC + cc)

    def plane_peer(dy, dx, dc=0):
        return device(lax.rem(y + dy, NY), lax.rem(x + dx, NX), z, lax.rem(core + dc, NC))

    core_peer = plane_peer(0, 0, 1)
    plane = [(dy, dx) for dy in far_first(NY) for dx in far_first(NX) if dy or dx]

    owners = min(OWNERS, replicas)
    first = (replicas - owners) // 2
    place = rep - first
    owns = (place >= 0) & (place < owners)

    def line_device(r, zz):
        return (r, device(y, x, zz, core)[1])

    def other(r, zz):
        return (rep != r) | (z != zz)

    tokens, width = tok.shape
    rows, heads = sum_ref.shape
    chunk = width // NY
    offs = far_first(NY)
    own = offs.index(0)
    x_rows = x1_out.shape[1]
    x_part, y_part = slice(0, x_rows), slice(x_rows, rows)

    arg_copies = [
        pltpu.make_async_copy(src, dst, arg_sem.at[i])
        for i, (src, dst) in enumerate(
            [(cot_hbm, cot), (mask_hbm, mask), (order_hbm, order), (loc_hbm.at[0], loc), (glob_hbm, glob)]
        )
    ]
    token_copies = [
        pltpu.make_async_copy(
            tok_hbm.at[pl.ds(i * TOKEN_BLOCK, TOKEN_BLOCK)],
            tok.at[pl.ds(i * TOKEN_BLOCK, TOKEN_BLOCK)],
            tok_sem.at[i],
        )
        for i in range(tokens // TOKEN_BLOCK)
    ]
    for copy in arg_copies + token_copies:
        copy.start()

    barrier = pltpu.get_barrier_semaphore()
    z_peer = line_device(rep, 1 - z)
    peers = [z_peer] + [plane_peer(*offset) for offset in plane] + [core_peer]
    for peer in peers:
        pl.semaphore_signal(barrier, inc=1, device_id=peer, device_id_type=MESH)
    for r in range(replicas):
        for zz in range(NZ):
            meets = rep != r
            if not first <= r < first + owners:
                meets = meets & owns

            @pl.when(meets)
            def _():
                pl.semaphore_signal(
                    barrier, inc=1, device_id=line_device(r, zz), device_id_type=MESH
                )

    line_count = NZ * jnp.where(owns, replicas - 1, owners)

    for copy in arg_copies:
        copy.wait()
    per_row = loc.shape[1] // LANES
    for i in range(FRAG):
        layer = order[i]
        diff = glob[pl.ds(layer, 1), :] - loc[pl.ds(layer, 1), :]
        for j in range(per_row):
            delta[i * per_row + j : i * per_row + j + 1, :] = diff[:, j * LANES : (j + 1) * LANES]

    cot_t = cot[...].astype(jnp.float32).T
    keep = jnp.broadcast_to(mask[...] == 1, cot_t.shape)
    masked[...] = jnp.where(keep, cot_t, 0.0).astype(jnp.bfloat16)

    for i, copy in enumerate(token_copies):
        copy.wait()
        for half in range(TOKEN_BLOCK // 16):
            at = pl.ds(i * TOKEN_BLOCK + half * 16, 16)
            sums = [jnp.zeros((16, LANES), jnp.float32) for _ in range(4)]
            for j in range(width // LANES):
                piece = tok[at, j * LANES : (j + 1) * LANES].astype(jnp.float32)
                sums[j % 4] += piece * piece
            total = jnp.sum((sums[0] + sums[1]) + (sums[2] + sums[3]), axis=1, keepdims=True)
            inv_rms = lax.rsqrt(total / width + EPSILON)
            for j in range(width // LANES):
                piece = tok[at, j * LANES : (j + 1) * LANES].astype(jnp.float32)
                tok[at, j * LANES : (j + 1) * LANES] = (piece * inv_rms).astype(jnp.bfloat16)

    def column(k):
        return lax.rem(y + offs[k], NY)

    def block_at(yy, xx, zz, cc):
        start = (((yy * NX + xx) * NZ + zz) * NC + cc) * rows
        return pl.multiple_of(start, 16)

    for k in range(NY):
        done = 0
        while done < chunk:
            size = min(256, chunk - done)
            at = pl.multiple_of(column(k) * chunk + done, LANES)
            product = jnp.dot(
                masked[...], tok[:, pl.ds(at, size)], preferred_element_type=jnp.float32
            )
            part[pl.ds(at, size), :] = product.T
            done += size
        for xx in range(NX):
            at = block_at(column(k), xx, 0, 1 - core)
            core_out[k, xx] = part[pl.ds(at, rows), :].astype(jnp.bfloat16)

    pl.semaphore_wait(barrier, len(peers) + line_count)

    sent = []

    def remote(src, dst, sems, out, into, peer):
        return pltpu.make_async_remote_copy(
            src_ref=src,
            dst_ref=dst,
            send_sem=sems.at[0, out],
            recv_sem=sems.at[1, into],
            device_id=peer,
            device_id_type=MESH,
        )

    def send(src, dst, sems, index, peer):
        copy = remote(src, dst, sems, index, index, peer)
        copy.start()
        sent.append(copy)
        return copy

    core_copies = {}
    for slot in range(NY):
        core_copies[slot] = send(core_out.at[slot], core_in.at[slot], core_sem, slot, core_peer)

    shard = delta.shape[0] // owners
    rs = [
        remote(
            delta.at[pl.ds(q * shard, shard)],
            delta_in.at[rep],
            rs_sem,
            q,
            rep,
            line_device(first + q, z),
        )
        for q in range(owners)
    ]
    rs_in = [
        remote(delta.at[pl.ds(0, shard)], delta_in.at[r], rs_sem, 0, r, z_peer)
        for r in range(replicas)
    ]

    def shard_at(q):
        return avg_ref.at[pl.ds(pl.multiple_of(q * shard, 8), shard)]

    ag = [
        remote(shard_at(place), shard_at(place), ag_sem, r, place, line_device(r, z))
        for r in range(replicas)
    ]
    ag_in = [
        remote(shard_at(q), shard_at(q), ag_sem, 0, q, z_peer) for q in range(owners)
    ]
    pair_copy = remote(
        sq_out.at[0], sq_plane.at[len(plane)], plane_sem, len(plane), len(plane), core_peer
    )
    plane_copies = [
        remote(sq_out.at[1], sq_plane.at[i], plane_sem, i, i, plane_peer(*offset))
        for i, offset in enumerate(plane)
    ]
    seat = place * NZ + z
    line = [
        remote(sq_out.at[2], sq_line.at[seat], line_sem, r * NZ + zz, seat, line_device(r, zz))
        for r in range(replicas)
        for zz in range(NZ)
    ]
    line_in = [
        remote(sq_out.at[2], sq_line.at[i], line_sem, 0, i, z_peer) for i in range(owners * NZ)
    ]

    for q in range(owners):

        @pl.when(rep != first + q)
        def _():
            rs[q].start()

    for k in range(NY):
        slot = NY + k
        for xx in range(NX):
            at = block_at(column(k), xx, 1, 1 - core)
            core_out[slot, xx] = part[pl.ds(at, rows), :].astype(jnp.bfloat16)
        core_copies[slot] = send(core_out.at[slot], core_in.at[slot], core_sem, slot, core_peer)

    def chip_sum(half, k, xx, at):
        start = block_at(column(k), xx, half, core) + at.start
        mine = part[pl.ds(start, at.stop - at.start), :]
        return mine + core_in[half * NY + k, xx, at].astype(jnp.float32)

    x1, y1, x2, y2 = {}, {}, {}, {}

    def x1_slot(half, k, off):
        return (half * NY + k) * (NX - 1) + off - 1

    def y_slot(half, off):
        return half * (NY - 1) + off - 1

    def x_slot(half, off):
        return half * (NX - 1) + off - 1

    def spread(half, k):
        core_copies[half * NY + k].wait_recv()
        for off in far_first(NX)[:-1]:
            slot = x1_slot(half, k, off)
            x1_out[slot] = chip_sum(half, k, lax.rem(x + off, NX), x_part).astype(jnp.bfloat16)
            x1[slot] = send(x1_out.at[slot], x1_in.at[slot], x1_sem, slot, plane_peer(0, off))
        if k != own:
            slot = y_slot(half, offs[k])
            for xx in range(NX):
                y1_out[slot, xx] = chip_sum(half, k, xx, y_part).astype(jnp.bfloat16)
            y1[slot] = send(
                y1_out.at[slot], y1_in.at[slot], y1_sem, slot, plane_peer(offs[k], 0)
            )

    def x_sum(half, k):
        total = chip_sum(half, k, x, x_part)
        for off in range(1, NX):
            slot = x1_slot(half, k, off)
            x1[slot].wait_recv()
            total = total + x1_in[slot].astype(jnp.float32)
        return total

    def y_sum(half, xx):
        total = chip_sum(half, own, xx, y_part)
        for off in range(1, NY):
            total = total + y1_in[y_slot(half, off), xx].astype(jnp.float32)
        return total

    def forward(half):
        for k in range(NY):
            if k != own:
                slot = y_slot(half, offs[k])
                x2_out[slot] = x_sum(half, k).astype(jnp.bfloat16)
                x2[slot] = send(
                    x2_out.at[slot], x2_in.at[slot], x2_sem, slot, plane_peer(offs[k], 0)
                )
        for off in range(1, NY):
            y1[y_slot(half, off)].wait_recv()
        for off in far_first(NX)[:-1]:
            slot = x_slot(half, off)
            y2_out[slot] = y_sum(half, lax.rem(x + off, NX)).astype(jnp.bfloat16)
            y2[slot] = send(y2_out.at[slot], y2_in.at[slot], y2_sem, slot, plane_peer(0, off))

    def gather(half):
        top = x_sum(half, own)
        low = y_sum(half, x)
        for off in range(1, NY):
            slot = y_slot(half, off)
            x2[slot].wait_recv()
            top = top + x2_in[slot].astype(jnp.float32)
        for off in range(1, NX):
            slot = x_slot(half, off)
            y2[slot].wait_recv()
            low = low + y2_in[slot].astype(jnp.float32)
        return top, low

    for k in range(NY):
        spread(0, k)

    @pl.when(owns)
    def _():
        delta_in[rep] = delta[pl.ds(pl.multiple_of(place * shard, 8), shard), :]
        for r in range(replicas):

            @pl.when(rep != r)
            def _():
                rs_in[r].wait_recv()

        total = delta_in[0]
        for r in range(1, replicas):
            total = total + delta_in[r]
        averaged = total / replicas
        avg_ref[pl.ds(pl.multiple_of(place * shard, 8), shard), :] = averaged
        sq_out[0] = jnp.sum(averaged * averaged, axis=0, keepdims=True)
        pair_copy.start()
        for r in range(replicas):

            @pl.when(rep != r)
            def _():
                ag[r].start()

        pair_copy.wait_recv()
        sq_out[1] = sq_out[0] + sq_plane[len(plane)]
        for copy in plane_copies:
            copy.start()

    forward(0)
    for k in range(NY):
        spread(1, k)

    @pl.when(owns)
    def _():
        squares = sq_out[1]
        for i, copy in enumerate(plane_copies):
            copy.wait_recv()
            squares = squares + sq_plane[i]
        sq_out[2] = squares
        sq_line[seat] = squares
        for r in range(replicas):
            for zz in range(NZ):

                @pl.when(other(r, zz))
                def _():
                    line[r * NZ + zz].start()

    z_copy = remote(z_out, z_in, z_sem, 0, 0, z_peer)

    def settle(half):
        top, low = gather(half)

        @pl.when(z == half)
        def _():
            sum_ref[x_part] = top
            sum_ref[y_part] = low

        @pl.when(z != half)
        def _():
            z_out[x_part] = top.astype(jnp.bfloat16)
            z_out[y_part] = low.astype(jnp.bfloat16)
            z_copy.start()

    settle(0)
    forward(1)
    settle(1)
    for q in range(owners):

        @pl.when(rep != first + q)
        def _():
            ag_in[q].wait_recv()

        for zz in range(NZ):

            @pl.when(other(first + q, zz))
            def _():
                line_in[q * NZ + zz].wait_recv()

    squares = sq_line[0]
    for i in range(1, owners * NZ):
        squares = squares + sq_line[i]
    sq_ref[...] = squares

    z_copy.wait_recv()
    sum_ref[...] = sum_ref[...] + z_in[...].astype(jnp.float32)
    z_copy.wait_send()
    for copy in sent:
        copy.wait_send()
    for q in range(owners):

        @pl.when(rep != first + q)
        def _():
            rs[q].wait_send()

    @pl.when(owns)
    def _():
        pair_copy.wait_send()
        for copy in plane_copies:
            copy.wait_send()
        for r in range(replicas):

            @pl.when(rep != r)
            def _():
                ag[r].wait_send()

            for zz in range(NZ):

                @pl.when(other(r, zz))
                def _():
                    line[r * NZ + zz].wait_send()


def exchange(tokens, cotangent, keep_mask, local_params, global_params, order, rows, replicas):
    count, width = tokens.shape
    heads = cotangent.shape[1]
    held, params = global_params.shape
    lines = FRAG * params // LANES
    vmem = pl.BlockSpec(memory_space=pltpu.VMEM)
    hbm = pl.BlockSpec(memory_space=pltpu.HBM)
    bf16, f32 = jnp.bfloat16, jnp.float32
    x_rows = (rows // 16 + 1) // 2 * 16
    x_block, y_block = (x_rows, heads), (rows - x_rows, heads)
    peers = NY * NX - 1
    owners = min(OWNERS, replicas)
    return pl.pallas_call(
        functools.partial(exchange_kernel, replicas),
        out_shape=(
            jax.ShapeDtypeStruct((rows, heads), f32),
            jax.ShapeDtypeStruct((lines, LANES), f32),
            jax.ShapeDtypeStruct((1, LANES), f32),
        ),
        in_specs=[hbm] * 6,
        out_specs=(vmem, vmem, vmem),
        scratch_shapes=[
            pltpu.VMEM((count, width), bf16),
            pltpu.VMEM((count, heads), bf16),
            pltpu.VMEM((1, count), jnp.int32),
            pltpu.VMEM((held, params), f32),
            pltpu.VMEM((held, params), f32),
            pltpu.SMEM(order.shape, jnp.int32),
            pltpu.VMEM((heads, count), bf16),
            pltpu.VMEM((width, heads), f32),
            pltpu.VMEM((2 * NY, NX, rows, heads), bf16),
            pltpu.VMEM((2 * NY, NX, rows, heads), bf16),
            pltpu.VMEM((2 * NY * (NX - 1),) + x_block, bf16),
            pltpu.VMEM((2 * NY * (NX - 1),) + x_block, bf16),
            pltpu.VMEM((2 * (NY - 1), NX) + y_block, bf16),
            pltpu.VMEM((2 * (NY - 1), NX) + y_block, bf16),
            pltpu.VMEM((2 * (NY - 1),) + x_block, bf16),
            pltpu.VMEM((2 * (NY - 1),) + x_block, bf16),
            pltpu.VMEM((2 * (NX - 1),) + y_block, bf16),
            pltpu.VMEM((2 * (NX - 1),) + y_block, bf16),
            pltpu.VMEM((rows, heads), bf16),
            pltpu.VMEM((rows, heads), bf16),
            pltpu.VMEM((lines, LANES), f32),
            pltpu.VMEM((replicas, lines // owners, LANES), f32),
            pltpu.VMEM((3, 1, LANES), f32),
            pltpu.VMEM((peers + 1, 1, LANES), f32),
            pltpu.VMEM((owners * NZ, 1, LANES), f32),
            pltpu.SemaphoreType.DMA((count // TOKEN_BLOCK,)),
            pltpu.SemaphoreType.DMA((5,)),
            pltpu.SemaphoreType.DMA((2, 2 * NY)),
            pltpu.SemaphoreType.DMA((2, 2 * NY * (NX - 1))),
            pltpu.SemaphoreType.DMA((2, 2 * (NY - 1))),
            pltpu.SemaphoreType.DMA((2, 2 * (NY - 1))),
            pltpu.SemaphoreType.DMA((2, 2 * (NX - 1))),
            pltpu.SemaphoreType.DMA((2, 1)),
            pltpu.SemaphoreType.DMA((2, replicas)),
            pltpu.SemaphoreType.DMA((2, replicas)),
            pltpu.SemaphoreType.DMA((2, peers + 1)),
            pltpu.SemaphoreType.DMA((2, replicas * NZ)),
        ],
        compiler_params=pltpu.CompilerParams(
            collective_id=0, has_side_effects=True, vmem_limit_bytes=63 * 1024 * 1024
        ),
        cost_estimate=pl.CostEstimate(
            flops=2 * count * width * heads, bytes_accessed=2 * count * width, transcendentals=0
        ),
    )(tokens, cotangent, keep_mask.reshape(1, count), local_params, global_params, order)


def finish_kernel(
    count,
    order_hbm,
    sum_hbm,
    avg_hbm,
    sq_hbm,
    weight_hbm,
    gain_hbm,
    loc_hbm,
    glob_hbm,
    mom_hbm,
    weight_out,
    gain_out,
    loc_out,
    glob_out,
    mom_out,
    order,
    total,
    avg,
    sq,
    weight,
    gain,
    loc,
    glob,
    mom,
    weight_new,
    gain_new,
    loc_new,
    glob_new,
    mom_new,
    in_sem,
    out_sem,
):
    pairs = [
        (avg_hbm, avg),
        (sq_hbm, sq),
        (loc_hbm.at[0], loc),
        (glob_hbm, glob),
        (mom_hbm, mom),
        (order_hbm, order),
        (sum_hbm, total),
        (weight_hbm.at[0], weight),
        (gain_hbm, gain),
    ]
    loads = [pltpu.make_async_copy(src, dst, in_sem.at[i]) for i, (src, dst) in enumerate(pairs)]
    for copy in loads:
        copy.start()
    for copy in loads:
        copy.wait()

    squares = jnp.sum(sq[...])
    limit = CLIP_RATE * jnp.sqrt(jnp.float32(count))
    factor = jnp.minimum(1.0, limit / jnp.sqrt(jnp.full((8, LANES), squares) + EPSILON))
    held, params = glob.shape
    layer = lax.broadcasted_iota(jnp.int32, (held, LANES), 0)
    first = layer == order[0]
    second = layer == order[1]
    picked = first | second
    lines = params // LANES
    stores = []

    def store(src, dst, index):
        copy = pltpu.make_async_copy(src, dst, out_sem.at[index])
        copy.start()
        stores.append(copy)

    parts = 2
    for part in range(parts):
        for j in range(part * lines // parts, (part + 1) * lines // parts):
            at = slice(j * LANES, (j + 1) * LANES)
            averaged = jnp.where(
                first,
                jnp.broadcast_to(avg[j : j + 1, :], (held, LANES)),
                jnp.broadcast_to(avg[lines + j : lines + j + 1, :], (held, LANES)),
            )
            old_loc, old_glob, old_mom = loc[:, at], glob[:, at], mom[:, at]
            clipped = averaged * factor
            moment_new = MOMENT * old_mom + clipped
            global_new = old_glob - OUTER_RATE * (clipped + MOMENT * moment_new)
            merged = MIX_RATE * old_loc + (1.0 - MIX_RATE) * global_new
            loc_new[:, at] = jnp.where(picked, merged, old_loc)
            glob_new[:, at] = jnp.where(picked, global_new, old_glob)
            mom_new[:, at] = jnp.where(picked, moment_new, old_mom)
        span = pl.ds(part * params // parts, params // parts)
        store(loc_new.at[:, span], loc_out.at[0, :, span], 3 * part)
        store(glob_new.at[:, span], glob_out.at[:, span], 3 * part + 1)
        store(mom_new.at[:, span], mom_out.at[:, span], 3 * part + 2)

    summed = total[...]
    rows, heads = summed.shape
    scale = jnp.broadcast_to(gain[...], (heads, rows)).T
    weight_new[...] = scale * summed
    store(weight_new, weight_out.at[0], 3 * parts)
    product = weight[...].astype(jnp.float32) * summed
    gain_new[...] = jnp.sum(product.T, axis=0, keepdims=True)
    store(gain_new, gain_out, 3 * parts + 1)
    for copy in stores:
        copy.wait()


def finish(order, total, averaged, squares, weight, gain, local_params, global_params, momentum, count):
    hbm = pl.BlockSpec(memory_space=pltpu.HBM)
    f32 = jnp.float32
    shapes = (
        jax.ShapeDtypeStruct(weight.shape, f32),
        jax.ShapeDtypeStruct(gain.shape, f32),
        jax.ShapeDtypeStruct(local_params.shape, f32),
        jax.ShapeDtypeStruct(global_params.shape, f32),
        jax.ShapeDtypeStruct(momentum.shape, f32),
    )
    state = pltpu.VMEM(global_params.shape, f32)
    return pl.pallas_call(
        functools.partial(finish_kernel, count),
        out_shape=shapes,
        in_specs=[hbm] * 9,
        out_specs=(hbm,) * 5,
        scratch_shapes=[
            pltpu.SMEM(order.shape, jnp.int32),
            pltpu.VMEM(total.shape, f32),
            pltpu.VMEM(averaged.shape, f32),
            pltpu.VMEM(squares.shape, f32),
            pltpu.VMEM(weight.shape[1:], weight.dtype),
            pltpu.VMEM(gain.shape, f32),
            state,
            state,
            state,
            pltpu.VMEM(weight.shape[1:], f32),
            pltpu.VMEM(gain.shape, f32),
            state,
            state,
            state,
            pltpu.SemaphoreType.DMA((9,)),
            pltpu.SemaphoreType.DMA((8,)),
        ],
        compiler_params=pltpu.CompilerParams(vmem_limit_bytes=63 * 1024 * 1024),
    )(order, total, averaged, squares, weight, gain, local_params, global_params, momentum)


def per_device(
    replicas,
    fsdp,
    tokens,
    cotangent,
    keep_mask,
    key_weight,
    norm_gain,
    local_params,
    global_params,
    momentum,
    fragment_order,
):
    total, averaged, squares = exchange(
        tokens,
        cotangent,
        keep_mask,
        local_params,
        global_params,
        fragment_order,
        key_weight.shape[1],
        replicas,
    )
    count = FRAG * global_params.shape[1] * fsdp
    return finish(
        fragment_order,
        total,
        averaged,
        squares,
        key_weight,
        norm_gain,
        local_params,
        global_params,
        momentum,
        count,
    )


def solution(mesh):
    in_specs = (
        P(("replica", "fsdp"), None),
        P(("replica", "fsdp"), None),
        P(("replica", "fsdp")),
        P("replica", "fsdp", None),
        P("replica", "fsdp"),
        P("replica", None, "fsdp"),
        P(None, "fsdp"),
        P(None, "fsdp"),
        P(),
    )
    out_specs = (
        P("replica", "fsdp", None),
        P("replica", "fsdp"),
        P("replica", None, "fsdp"),
        P(None, "fsdp"),
        P(None, "fsdp"),
    )
    return jax.shard_map(
        functools.partial(per_device, mesh.shape["replica"], mesh.shape["fsdp"]),
        mesh=mesh,
        in_specs=in_specs,
        out_specs=out_specs,
        check_vma=False,
    )
```

```python
import functools

import jax
import jax.numpy as jnp
from jax import lax
from jax.experimental import pallas as pl
from jax.experimental.pallas import tpu as pltpu
from jax.sharding import PartitionSpec as P

FRAG = 2

EPSILON = 1e-06
CLIP_RATE = 0.5
MOMENT = 0.9
OUTER_RATE = 0.7
MIX_RATE = 0.5

NY, NX, NZ, NC = 4, 4, 2, 2
LANES = 128
TOKEN_BLOCK = 32
TOKEN_WINDOW = 5
OWNERS = 4
MESH = pl.DeviceIdType.MESH


def far_first(count):
    return sorted(range(count), key=lambda off: (-min(off, count - off), off))


def exchange_kernel(
    replicas,
    tok_hbm,
    cot_hbm,
    mask_hbm,
    loc_hbm,
    glob_hbm,
    order_hbm,
    sum_ref,
    avg_ref,
    sq_ref,
    tok,
    cot,
    mask,
    loc,
    glob,
    order,
    masked,
    part,
    core_out,
    core_in,
    x1_out,
    x1_in,
    y1_out,
    y1_in,
    x2_out,
    x2_in,
    y2_out,
    y2_in,
    z_out,
    z_in,
    delta,
    delta_in,
    sq_out,
    sq_plane,
    sq_line,
    tok_sem,
    arg_sem,
    core_sem,
    x1_sem,
    y1_sem,
    x2_sem,
    y2_sem,
    z_sem,
    rs_sem,
    ag_sem,
    plane_sem,
    line_sem,
):
    rep = lax.axis_index("replica")
    me = lax.axis_index("fsdp")
    core = lax.rem(me, NC)
    z = lax.rem(me // NC, NZ)
    x = lax.rem(me // (NC * NZ), NX)
    y = me // (NC * NZ * NX)

    def device(yy, xx, zz, cc):
        return (rep, ((yy * NX + xx) * NZ + zz) * NC + cc)

    def plane_peer(dy, dx, dc=0):
        return device(lax.rem(y + dy, NY), lax.rem(x + dx, NX), z, lax.rem(core + dc, NC))

    core_peer = plane_peer(0, 0, 1)
    plane = [(dy, dx) for dy in far_first(NY) for dx in far_first(NX) if dy or dx]

    owners = min(OWNERS, replicas)
    first = (replicas - owners) // 2
    place = rep - first
    owns = (place >= 0) & (place < owners)

    def line_device(r, zz):
        return (r, device(y, x, zz, core)[1])

    def other(r, zz):
        return (rep != r) | (z != zz)

    tokens, width = tok.shape
    rows, heads = sum_ref.shape
    chunk = width // NY
    offs = far_first(NY)
    own = offs.index(0)
    x_rows = x1_out.shape[1]
    x_part, y_part = slice(0, x_rows), slice(x_rows, rows)

    arg_copies = [
        pltpu.make_async_copy(src, dst, arg_sem.at[i])
        for i, (src, dst) in enumerate(
            [(cot_hbm, cot), (mask_hbm, mask), (order_hbm, order), (loc_hbm.at[0], loc), (glob_hbm, glob)]
        )
    ]
    token_copies = [
        pltpu.make_async_copy(
            tok_hbm.at[pl.ds(i * TOKEN_BLOCK, TOKEN_BLOCK)],
            tok.at[pl.ds(i * TOKEN_BLOCK, TOKEN_BLOCK)],
            tok_sem.at[i],
        )
        for i in range(tokens // TOKEN_BLOCK)
    ]
    for copy in arg_copies + token_copies[:TOKEN_WINDOW]:
        copy.start()

    barrier = pltpu.get_barrier_semaphore()
    z_peer = line_device(rep, 1 - z)
    peers = [z_peer] + [plane_peer(*offset) for offset in plane] + [core_peer]
    for peer in peers:
        pl.semaphore_signal(barrier, inc=1, device_id=peer, device_id_type=MESH)
    for r in range(replicas):
        for zz in range(NZ):
            meets = rep != r
            if not first <= r < first + owners:
                meets = meets & owns

            @pl.when(meets)
            def _():
                pl.semaphore_signal(
                    barrier, inc=1, device_id=line_device(r, zz), device_id_type=MESH
                )

    line_count = NZ * jnp.where(owns, replicas - 1, owners)

    for copy in arg_copies:
        copy.wait()
    per_row = loc.shape[1] // LANES
    for i in range(FRAG):
        layer = order[i]
        diff = glob[pl.ds(layer, 1), :] - loc[pl.ds(layer, 1), :]
        for j in range(per_row):
            delta[i * per_row + j : i * per_row + j + 1, :] = diff[:, j * LANES : (j + 1) * LANES]

    cot_t = cot[...].astype(jnp.float32).T
    keep = jnp.broadcast_to(mask[...] == 1, cot_t.shape)
    masked[...] = jnp.where(keep, cot_t, 0.0).astype(jnp.bfloat16)

    for i, copy in enumerate(token_copies):
        copy.wait()
        if i + TOKEN_WINDOW < len(token_copies):
            token_copies[i + TOKEN_WINDOW].start()
        for half in range(TOKEN_BLOCK // 16):
            at = pl.ds(i * TOKEN_BLOCK + half * 16, 16)
            sums = [jnp.zeros((16, LANES), jnp.float32) for _ in range(4)]
            for j in range(width // LANES):
                piece = tok[at, j * LANES : (j + 1) * LANES].astype(jnp.float32)
                sums[j % 4] += piece * piece
            total = jnp.sum((sums[0] + sums[1]) + (sums[2] + sums[3]), axis=1, keepdims=True)
            inv_rms = lax.rsqrt(total / width + EPSILON)
            for j in range(width // LANES):
                piece = tok[at, j * LANES : (j + 1) * LANES].astype(jnp.float32)
                tok[at, j * LANES : (j + 1) * LANES] = (piece * inv_rms).astype(jnp.bfloat16)

    def column(k):
        return lax.rem(y + offs[k], NY)

    def block_at(yy, xx, zz, cc):
        start = (((yy * NX + xx) * NZ + zz) * NC + cc) * rows
        return pl.multiple_of(start, 16)

    for k in range(NY):
        done = 0
        while done < chunk:
            size = min(256, chunk - done)
            at = pl.multiple_of(column(k) * chunk + done, LANES)
            product = jnp.dot(
                masked[...], tok[:, pl.ds(at, size)], preferred_element_type=jnp.float32
            )
            part[pl.ds(at, size), :] = product.T
            done += size
        for xx in range(NX):
            at = block_at(column(k), xx, 0, 1 - core)
            core_out[k, xx] = part[pl.ds(at, rows), :].astype(jnp.bfloat16)

    pl.semaphore_wait(barrier, len(peers) + line_count)

    sent = []

    def remote(src, dst, sems, out, into, peer):
        return pltpu.make_async_remote_copy(
            src_ref=src,
            dst_ref=dst,
            send_sem=sems.at[0, out],
            recv_sem=sems.at[1, into],
            device_id=peer,
            device_id_type=MESH,
        )

    def send(src, dst, sems, index, peer):
        copy = remote(src, dst, sems, index, index, peer)
        copy.start()
        sent.append(copy)
        return copy

    core_copies = {}
    for slot in range(NY):
        core_copies[slot] = send(core_out.at[slot], core_in.at[slot], core_sem, slot, core_peer)

    shard = delta.shape[0] // owners
    rs = [
        remote(
            delta.at[pl.ds(q * shard, shard)],
            delta_in.at[rep],
            rs_sem,
            q,
            rep,
            line_device(first + q, z),
        )
        for q in range(owners)
    ]
    rs_in = [
        remote(delta.at[pl.ds(0, shard)], delta_in.at[r], rs_sem, 0, r, z_peer)
        for r in range(replicas)
    ]

    def shard_at(q):
        return avg_ref.at[pl.ds(pl.multiple_of(q * shard, 8), shard)]

    ag = [
        remote(shard_at(place), shard_at(place), ag_sem, r, place, line_device(r, z))
        for r in range(replicas)
    ]
    ag_in = [
        remote(shard_at(q), shard_at(q), ag_sem, 0, q, z_peer) for q in range(owners)
    ]
    pair_copy = remote(
        sq_out.at[0], sq_plane.at[len(plane)], plane_sem, len(plane), len(plane), core_peer
    )
    plane_copies = [
        remote(sq_out.at[1], sq_plane.at[i], plane_sem, i, i, plane_peer(*offset))
        for i, offset in enumerate(plane)
    ]
    seat = place * NZ + z
    line = [
        remote(sq_out.at[2], sq_line.at[seat], line_sem, r * NZ + zz, seat, line_device(r, zz))
        for r in range(replicas)
        for zz in range(NZ)
    ]
    line_in = [
        remote(sq_out.at[2], sq_line.at[i], line_sem, 0, i, z_peer) for i in range(owners * NZ)
    ]

    for q in range(owners):

        @pl.when(rep != first + q)
        def _():
            rs[q].start()

    for k in range(NY):
        slot = NY + k
        for xx in range(NX):
            at = block_at(column(k), xx, 1, 1 - core)
            core_out[slot, xx] = part[pl.ds(at, rows), :].astype(jnp.bfloat16)
        core_copies[slot] = send(core_out.at[slot], core_in.at[slot], core_sem, slot, core_peer)

    def chip_sum(half, k, xx, at):
        start = block_at(column(k), xx, half, core) + at.start
        mine = part[pl.ds(start, at.stop - at.start), :]
        return mine + core_in[half * NY + k, xx, at].astype(jnp.float32)

    x1, y1, x2, y2 = {}, {}, {}, {}

    def x1_slot(half, k, off):
        return (half * NY + k) * (NX - 1) + off - 1

    def y_slot(half, off):
        return half * (NY - 1) + off - 1

    def x_slot(half, off):
        return half * (NX - 1) + off - 1

    def spread(half, k):
        core_copies[half * NY + k].wait_recv()
        for off in far_first(NX)[:-1]:
            slot = x1_slot(half, k, off)
            x1_out[slot] = chip_sum(half, k, lax.rem(x + off, NX), x_part).astype(jnp.bfloat16)
            x1[slot] = send(x1_out.at[slot], x1_in.at[slot], x1_sem, slot, plane_peer(0, off))
        if k != own:
            slot = y_slot(half, offs[k])
            for xx in range(NX):
                y1_out[slot, xx] = chip_sum(half, k, xx, y_part).astype(jnp.bfloat16)
            y1[slot] = send(
                y1_out.at[slot], y1_in.at[slot], y1_sem, slot, plane_peer(offs[k], 0)
            )

    def x_sum(half, k):
        total = chip_sum(half, k, x, x_part)
        for off in range(1, NX):
            slot = x1_slot(half, k, off)
            x1[slot].wait_recv()
            total = total + x1_in[slot].astype(jnp.float32)
        return total

    def y_sum(half, xx):
        total = chip_sum(half, own, xx, y_part)
        for off in range(1, NY):
            total = total + y1_in[y_slot(half, off), xx].astype(jnp.float32)
        return total

    def forward(half):
        for k in range(NY):
            if k != own:
                slot = y_slot(half, offs[k])
                x2_out[slot] = x_sum(half, k).astype(jnp.bfloat16)
                x2[slot] = send(
                    x2_out.at[slot], x2_in.at[slot], x2_sem, slot, plane_peer(offs[k], 0)
                )
        for off in range(1, NY):
            y1[y_slot(half, off)].wait_recv()
        for off in far_first(NX)[:-1]:
            slot = x_slot(half, off)
            y2_out[slot] = y_sum(half, lax.rem(x + off, NX)).astype(jnp.bfloat16)
            y2[slot] = send(y2_out.at[slot], y2_in.at[slot], y2_sem, slot, plane_peer(0, off))

    def gather(half):
        top = x_sum(half, own)
        low = y_sum(half, x)
        for off in range(1, NY):
            slot = y_slot(half, off)
            x2[slot].wait_recv()
            top = top + x2_in[slot].astype(jnp.float32)
        for off in range(1, NX):
            slot = x_slot(half, off)
            y2[slot].wait_recv()
            low = low + y2_in[slot].astype(jnp.float32)
        return top, low

    for k in range(NY):
        spread(0, k)

    @pl.when(owns)
    def _():
        delta_in[rep] = delta[pl.ds(pl.multiple_of(place * shard, 8), shard), :]
        for r in range(replicas):

            @pl.when(rep != r)
            def _():
                rs_in[r].wait_recv()

        total = delta_in[0]
        for r in range(1, replicas):
            total = total + delta_in[r]
        averaged = total / replicas
        avg_ref[pl.ds(pl.multiple_of(place * shard, 8), shard), :] = averaged
        sq_out[0] = jnp.sum(averaged * averaged, axis=0, keepdims=True)
        pair_copy.start()
        for r in range(replicas):

            @pl.when(rep != r)
            def _():
                ag[r].start()

        pair_copy.wait_recv()
        sq_out[1] = sq_out[0] + sq_plane[len(plane)]
        for copy in plane_copies:
            copy.start()

    forward(0)
    for k in range(NY):
        spread(1, k)

    @pl.when(owns)
    def _():
        squares = sq_out[1]
        for i, copy in enumerate(plane_copies):
            copy.wait_recv()
            squares = squares + sq_plane[i]
        sq_out[2] = squares
        sq_line[seat] = squares
        for r in range(replicas):
            for zz in range(NZ):

                @pl.when(other(r, zz))
                def _():
                    line[r * NZ + zz].start()

    z_copy = remote(z_out, z_in, z_sem, 0, 0, z_peer)

    def settle(half):
        top, low = gather(half)

        @pl.when(z == half)
        def _():
            sum_ref[x_part] = top
            sum_ref[y_part] = low

        @pl.when(z != half)
        def _():
            z_out[x_part] = top.astype(jnp.bfloat16)
            z_out[y_part] = low.astype(jnp.bfloat16)
            z_copy.start()

    settle(0)
    forward(1)
    settle(1)
    for q in range(owners):

        @pl.when(rep != first + q)
        def _():
            ag_in[q].wait_recv()

        for zz in range(NZ):

            @pl.when(other(first + q, zz))
            def _():
                line_in[q * NZ + zz].wait_recv()

    squares = sq_line[0]
    for i in range(1, owners * NZ):
        squares = squares + sq_line[i]
    sq_ref[...] = squares

    for copy in sent:
        copy.wait_send()
    for q in range(owners):

        @pl.when(rep != first + q)
        def _():
            rs[q].wait_send()

    @pl.when(owns)
    def _():
        pair_copy.wait_send()
        for copy in plane_copies:
            copy.wait_send()
        for r in range(replicas):

            @pl.when(rep != r)
            def _():
                ag[r].wait_send()

            for zz in range(NZ):

                @pl.when(other(r, zz))
                def _():
                    line[r * NZ + zz].wait_send()

    z_copy.wait_recv()
    sum_ref[...] = sum_ref[...] + z_in[...].astype(jnp.float32)
    z_copy.wait_send()


def exchange(tokens, cotangent, keep_mask, local_params, global_params, order, rows, replicas):
    count, width = tokens.shape
    heads = cotangent.shape[1]
    held, params = global_params.shape
    lines = FRAG * params // LANES
    vmem = pl.BlockSpec(memory_space=pltpu.VMEM)
    hbm = pl.BlockSpec(memory_space=pltpu.HBM)
    bf16, f32 = jnp.bfloat16, jnp.float32
    x_rows = (rows // 16 + 1) // 2 * 16
    x_block, y_block = (x_rows, heads), (rows - x_rows, heads)
    peers = NY * NX - 1
    owners = min(OWNERS, replicas)
    return pl.pallas_call(
        functools.partial(exchange_kernel, replicas),
        out_shape=(
            jax.ShapeDtypeStruct((rows, heads), f32),
            jax.ShapeDtypeStruct((lines, LANES), f32),
            jax.ShapeDtypeStruct((1, LANES), f32),
        ),
        in_specs=[hbm] * 6,
        out_specs=(vmem, vmem, vmem),
        scratch_shapes=[
            pltpu.VMEM((count, width), bf16),
            pltpu.VMEM((count, heads), bf16),
            pltpu.VMEM((1, count), jnp.int32),
            pltpu.VMEM((held, params), f32),
            pltpu.VMEM((held, params), f32),
            pltpu.SMEM(order.shape, jnp.int32),
            pltpu.VMEM((heads, count), bf16),
            pltpu.VMEM((width, heads), f32),
            pltpu.VMEM((2 * NY, NX, rows, heads), bf16),
            pltpu.VMEM((2 * NY, NX, rows, heads), bf16),
            pltpu.VMEM((2 * NY * (NX - 1),) + x_block, bf16),
            pltpu.VMEM((2 * NY * (NX - 1),) + x_block, bf16),
            pltpu.VMEM((2 * (NY - 1), NX) + y_block, bf16),
            pltpu.VMEM((2 * (NY - 1), NX) + y_block, bf16),
            pltpu.VMEM((2 * (NY - 1),) + x_block, bf16),
            pltpu.VMEM((2 * (NY - 1),) + x_block, bf16),
            pltpu.VMEM((2 * (NX - 1),) + y_block, bf16),
            pltpu.VMEM((2 * (NX - 1),) + y_block, bf16),
            pltpu.VMEM((rows, heads), bf16),
            pltpu.VMEM((rows, heads), bf16),
            pltpu.VMEM((lines, LANES), f32),
            pltpu.VMEM((replicas, lines // owners, LANES), f32),
            pltpu.VMEM((3, 1, LANES), f32),
            pltpu.VMEM((peers + 1, 1, LANES), f32),
            pltpu.VMEM((owners * NZ, 1, LANES), f32),
            pltpu.SemaphoreType.DMA((count // TOKEN_BLOCK,)),
            pltpu.SemaphoreType.DMA((5,)),
            pltpu.SemaphoreType.DMA((2, 2 * NY)),
            pltpu.SemaphoreType.DMA((2, 2 * NY * (NX - 1))),
            pltpu.SemaphoreType.DMA((2, 2 * (NY - 1))),
            pltpu.SemaphoreType.DMA((2, 2 * (NY - 1))),
            pltpu.SemaphoreType.DMA((2, 2 * (NX - 1))),
            pltpu.SemaphoreType.DMA((2, 1)),
            pltpu.SemaphoreType.DMA((2, replicas)),
            pltpu.SemaphoreType.DMA((2, replicas)),
            pltpu.SemaphoreType.DMA((2, peers + 1)),
            pltpu.SemaphoreType.DMA((2, replicas * NZ)),
        ],
        compiler_params=pltpu.CompilerParams(
            collective_id=0, has_side_effects=True, vmem_limit_bytes=63 * 1024 * 1024
        ),
        cost_estimate=pl.CostEstimate(
            flops=2 * count * width * heads, bytes_accessed=2 * count * width, transcendentals=0
        ),
    )(tokens, cotangent, keep_mask.reshape(1, count), local_params, global_params, order)


def finish_kernel(
    count,
    order_hbm,
    sum_hbm,
    avg_hbm,
    sq_hbm,
    weight_hbm,
    gain_hbm,
    loc_hbm,
    glob_hbm,
    mom_hbm,
    weight_out,
    gain_out,
    loc_out,
    glob_out,
    mom_out,
    order,
    total,
    avg,
    sq,
    weight,
    gain,
    loc,
    glob,
    mom,
    weight_new,
    gain_new,
    loc_new,
    glob_new,
    mom_new,
    in_sem,
    out_sem,
):
    pairs = [
        (avg_hbm, avg),
        (sq_hbm, sq),
        (loc_hbm.at[0], loc),
        (glob_hbm, glob),
        (mom_hbm, mom),
        (order_hbm, order),
        (sum_hbm, total),
        (weight_hbm.at[0], weight),
        (gain_hbm, gain),
    ]
    loads = [pltpu.make_async_copy(src, dst, in_sem.at[i]) for i, (src, dst) in enumerate(pairs)]
    for copy in loads:
        copy.start()
    for copy in loads:
        copy.wait()

    squares = jnp.sum(sq[...])
    limit = CLIP_RATE * jnp.sqrt(jnp.float32(count))
    factor = jnp.minimum(1.0, limit / jnp.sqrt(jnp.full((8, LANES), squares) + EPSILON))
    held, params = glob.shape
    layer = lax.broadcasted_iota(jnp.int32, (held, LANES), 0)
    first = layer == order[0]
    second = layer == order[1]
    picked = first | second
    lines = params // LANES
    stores = []

    def store(src, dst, index):
        copy = pltpu.make_async_copy(src, dst, out_sem.at[index])
        copy.start()
        stores.append(copy)

    parts = 2
    for part in range(parts):
        for j in range(part * lines // parts, (part + 1) * lines // parts):
            at = slice(j * LANES, (j + 1) * LANES)
            averaged = jnp.where(
                first,
                jnp.broadcast_to(avg[j : j + 1, :], (held, LANES)),
                jnp.broadcast_to(avg[lines + j : lines + j + 1, :], (held, LANES)),
            )
            old_loc, old_glob, old_mom = loc[:, at], glob[:, at], mom[:, at]
            clipped = averaged * factor
            moment_new = MOMENT * old_mom + clipped
            global_new = old_glob - OUTER_RATE * (clipped + MOMENT * moment_new)
            merged = MIX_RATE * old_loc + (1.0 - MIX_RATE) * global_new
            loc_new[:, at] = jnp.where(picked, merged, old_loc)
            glob_new[:, at] = jnp.where(picked, global_new, old_glob)
            mom_new[:, at] = jnp.where(picked, moment_new, old_mom)
        span = pl.ds(part * params // parts, params // parts)
        store(loc_new.at[:, span], loc_out.at[0, :, span], 3 * part)
        store(glob_new.at[:, span], glob_out.at[:, span], 3 * part + 1)
        store(mom_new.at[:, span], mom_out.at[:, span], 3 * part + 2)

    summed = total[...]
    rows, heads = summed.shape
    scale = jnp.broadcast_to(gain[...], (heads, rows)).T
    weight_new[...] = scale * summed
    store(weight_new, weight_out.at[0], 3 * parts)
    product = weight[...].astype(jnp.float32) * summed
    gain_new[...] = jnp.sum(product.T, axis=0, keepdims=True)
    store(gain_new, gain_out, 3 * parts + 1)
    for copy in stores:
        copy.wait()


def finish(order, total, averaged, squares, weight, gain, local_params, global_params, momentum, count):
    hbm = pl.BlockSpec(memory_space=pltpu.HBM)
    f32 = jnp.float32
    shapes = (
        jax.ShapeDtypeStruct(weight.shape, f32),
        jax.ShapeDtypeStruct(gain.shape, f32),
        jax.ShapeDtypeStruct(local_params.shape, f32),
        jax.ShapeDtypeStruct(global_params.shape, f32),
        jax.ShapeDtypeStruct(momentum.shape, f32),
    )
    state = pltpu.VMEM(global_params.shape, f32)
    return pl.pallas_call(
        functools.partial(finish_kernel, count),
        out_shape=shapes,
        in_specs=[hbm] * 9,
        out_specs=(hbm,) * 5,
        scratch_shapes=[
            pltpu.SMEM(order.shape, jnp.int32),
            pltpu.VMEM(total.shape, f32),
            pltpu.VMEM(averaged.shape, f32),
            pltpu.VMEM(squares.shape, f32),
            pltpu.VMEM(weight.shape[1:], weight.dtype),
            pltpu.VMEM(gain.shape, f32),
            state,
            state,
            state,
            pltpu.VMEM(weight.shape[1:], f32),
            pltpu.VMEM(gain.shape, f32),
            state,
            state,
            state,
            pltpu.SemaphoreType.DMA((9,)),
            pltpu.SemaphoreType.DMA((8,)),
        ],
        compiler_params=pltpu.CompilerParams(vmem_limit_bytes=63 * 1024 * 1024),
    )(order, total, averaged, squares, weight, gain, local_params, global_params, momentum)


def per_device(
    replicas,
    fsdp,
    tokens,
    cotangent,
    keep_mask,
    key_weight,
    norm_gain,
    local_params,
    global_params,
    momentum,
    fragment_order,
):
    total, averaged, squares = exchange(
        tokens,
        cotangent,
        keep_mask,
        local_params,
        global_params,
        fragment_order,
        key_weight.shape[1],
        replicas,
    )
    count = FRAG * global_params.shape[1] * fsdp
    return finish(
        fragment_order,
        total,
        averaged,
        squares,
        key_weight,
        norm_gain,
        local_params,
        global_params,
        momentum,
        count,
    )


def solution(mesh):
    in_specs = (
        P(("replica", "fsdp"), None),
        P(("replica", "fsdp"), None),
        P(("replica", "fsdp")),
        P("replica", "fsdp", None),
        P("replica", "fsdp"),
        P("replica", None, "fsdp"),
        P(None, "fsdp"),
        P(None, "fsdp"),
        P(),
    )
    out_specs = (
        P("replica", "fsdp", None),
        P("replica", "fsdp"),
        P("replica", None, "fsdp"),
        P(None, "fsdp"),
        P(None, "fsdp"),
    )
    return jax.shard_map(
        functools.partial(per_device, mesh.shape["replica"], mesh.shape["fsdp"]),
        mesh=mesh,
        in_specs=in_specs,
        out_specs=out_specs,
        check_vma=False,
    )
```

```python
import functools

import jax
import jax.numpy as jnp
from jax import lax
from jax.experimental import pallas as pl
from jax.experimental.pallas import tpu as pltpu
from jax.sharding import PartitionSpec as P

FRAG = 2

EPSILON = 1e-06
CLIP_RATE = 0.5
MOMENT = 0.9
OUTER_RATE = 0.7
MIX_RATE = 0.5

NY, NX, NZ, NC = 4, 4, 2, 2
LANES = 128
TOKEN_BLOCK = 32
TOKEN_WINDOW = 5
OWNERS = 4
MESH = pl.DeviceIdType.MESH


def far_first(count):
    return sorted(range(count), key=lambda off: (-min(off, count - off), off))


def exchange_kernel(
    replicas,
    tok_hbm,
    cot_hbm,
    mask_hbm,
    loc_hbm,
    glob_hbm,
    order_hbm,
    sum_ref,
    avg_ref,
    sq_ref,
    tok,
    cot,
    mask,
    loc,
    glob,
    order,
    masked,
    part,
    core_out,
    core_in,
    x1_out,
    x1_in,
    y1_out,
    y1_in,
    x2_out,
    x2_in,
    y2_out,
    y2_in,
    z_out,
    z_in,
    delta,
    delta_in,
    sq_out,
    sq_plane,
    sq_line,
    tok_sem,
    arg_sem,
    core_sem,
    x1_sem,
    y1_sem,
    x2_sem,
    y2_sem,
    z_sem,
    rs_sem,
    ag_sem,
    plane_sem,
    line_sem,
):
    rep = lax.axis_index("replica")
    me = lax.axis_index("fsdp")
    core = lax.rem(me, NC)
    z = lax.rem(me // NC, NZ)
    x = lax.rem(me // (NC * NZ), NX)
    y = me // (NC * NZ * NX)

    def device(yy, xx, zz, cc):
        return (rep, ((yy * NX + xx) * NZ + zz) * NC + cc)

    def plane_peer(dy, dx, dc=0):
        return device(lax.rem(y + dy, NY), lax.rem(x + dx, NX), z, lax.rem(core + dc, NC))

    core_peer = plane_peer(0, 0, 1)
    plane = [(dy, dx) for dy in far_first(NY) for dx in far_first(NX) if dy or dx]

    owners = min(OWNERS, replicas)
    first = (replicas - owners) // 2
    owns = (rep >= first) & (rep < first + owners)
    place = lax.rem(rep - first + owners * replicas, owners)

    def line_device(r, zz):
        return (r, device(y, x, zz, core)[1])

    def other(r, zz):
        return (rep != r) | (z != zz)

    tokens, width = tok.shape
    rows, heads = sum_ref.shape
    chunk = width // NY
    offs = far_first(NY)
    own = offs.index(0)
    x_rows = x1_out.shape[1]
    x_part, y_part = slice(0, x_rows), slice(x_rows, rows)

    arg_copies = [
        pltpu.make_async_copy(src, dst, arg_sem.at[i])
        for i, (src, dst) in enumerate(
            [(cot_hbm, cot), (mask_hbm, mask), (order_hbm, order), (loc_hbm.at[0], loc), (glob_hbm, glob)]
        )
    ]
    token_copies = [
        pltpu.make_async_copy(
            tok_hbm.at[pl.ds(i * TOKEN_BLOCK, TOKEN_BLOCK)],
            tok.at[pl.ds(i * TOKEN_BLOCK, TOKEN_BLOCK)],
            tok_sem.at[i],
        )
        for i in range(tokens // TOKEN_BLOCK)
    ]
    for copy in arg_copies + token_copies[:TOKEN_WINDOW]:
        copy.start()

    barrier = pltpu.get_barrier_semaphore()
    z_peer = line_device(rep, 1 - z)
    peers = [z_peer] + [plane_peer(*offset) for offset in plane] + [core_peer]
    for peer in peers:
        pl.semaphore_signal(barrier, inc=1, device_id=peer, device_id_type=MESH)
    for r in range(replicas):
        for zz in range(NZ):
            meets = rep != r
            if not first <= r < first + owners:
                meets = meets & owns

            @pl.when(meets)
            def _():
                pl.semaphore_signal(
                    barrier, inc=1, device_id=line_device(r, zz), device_id_type=MESH
                )

    line_count = NZ * jnp.where(owns, replicas - 1, owners)

    for copy in arg_copies:
        copy.wait()
    per_row = loc.shape[1] // LANES
    for i in range(FRAG):
        layer = order[i]
        diff = glob[pl.ds(layer, 1), :] - loc[pl.ds(layer, 1), :]
        for j in range(per_row):
            delta[i * per_row + j : i * per_row + j + 1, :] = diff[:, j * LANES : (j + 1) * LANES]

    cot_t = cot[...].astype(jnp.float32).T
    keep = jnp.broadcast_to(mask[...] == 1, cot_t.shape)
    masked[...] = jnp.where(keep, cot_t, 0.0).astype(jnp.bfloat16)

    for i, copy in enumerate(token_copies):
        copy.wait()
        if i + TOKEN_WINDOW < len(token_copies):
            token_copies[i + TOKEN_WINDOW].start()
        for half in range(TOKEN_BLOCK // 16):
            at = pl.ds(i * TOKEN_BLOCK + half * 16, 16)
            sums = [jnp.zeros((16, LANES), jnp.float32) for _ in range(4)]
            for j in range(width // LANES):
                piece = tok[at, j * LANES : (j + 1) * LANES].astype(jnp.float32)
                sums[j % 4] += piece * piece
            total = jnp.sum((sums[0] + sums[1]) + (sums[2] + sums[3]), axis=1, keepdims=True)
            inv_rms = lax.rsqrt(total / width + EPSILON)
            for j in range(width // LANES):
                piece = tok[at, j * LANES : (j + 1) * LANES].astype(jnp.float32)
                tok[at, j * LANES : (j + 1) * LANES] = (piece * inv_rms).astype(jnp.bfloat16)

    def column(k):
        return lax.rem(y + offs[k], NY)

    def block_at(yy, xx, zz, cc):
        start = (((yy * NX + xx) * NZ + zz) * NC + cc) * rows
        return pl.multiple_of(start, 16)

    for k in range(NY):
        done = 0
        while done < chunk:
            size = min(256, chunk - done)
            at = pl.multiple_of(column(k) * chunk + done, LANES)
            product = jnp.dot(
                masked[...], tok[:, pl.ds(at, size)], preferred_element_type=jnp.float32
            )
            part[pl.ds(at, size), :] = product.T
            done += size
        for xx in range(NX):
            at = block_at(column(k), xx, 0, 1 - core)
            core_out[k, xx] = part[pl.ds(at, rows), :].astype(jnp.bfloat16)

    pl.semaphore_wait(barrier, len(peers) + line_count)

    sent = []

    def remote(src, dst, sems, out, into, peer):
        return pltpu.make_async_remote_copy(
            src_ref=src,
            dst_ref=dst,
            send_sem=sems.at[0, out],
            recv_sem=sems.at[1, into],
            device_id=peer,
            device_id_type=MESH,
        )

    def send(src, dst, sems, index, peer):
        copy = remote(src, dst, sems, index, index, peer)
        copy.start()
        sent.append(copy)
        return copy

    core_copies = {}
    for slot in range(NY):
        core_copies[slot] = send(core_out.at[slot], core_in.at[slot], core_sem, slot, core_peer)

    shard = delta.shape[0] // owners
    rs = [
        remote(
            delta.at[pl.ds(q * shard, shard)],
            delta_in.at[rep],
            rs_sem,
            q,
            rep,
            line_device(first + q, z),
        )
        for q in range(owners)
    ]
    rs_in = [
        remote(delta.at[pl.ds(0, shard)], delta_in.at[r], rs_sem, 0, r, z_peer)
        for r in range(replicas)
    ]

    def shard_at(q):
        return avg_ref.at[pl.ds(pl.multiple_of(q * shard, 8), shard)]

    ag = [
        remote(shard_at(place), shard_at(place), ag_sem, r, place, line_device(r, z))
        for r in range(replicas)
    ]
    ag_in = [
        remote(shard_at(q), shard_at(q), ag_sem, 0, q, z_peer) for q in range(owners)
    ]
    pair_copy = remote(
        sq_out.at[0], sq_plane.at[len(plane)], plane_sem, len(plane), len(plane), core_peer
    )
    plane_copies = [
        remote(sq_out.at[1], sq_plane.at[i], plane_sem, i, i, plane_peer(*offset))
        for i, offset in enumerate(plane)
    ]
    seat = place * NZ + z
    line = [
        remote(sq_out.at[2], sq_line.at[seat], line_sem, r * NZ + zz, seat, line_device(r, zz))
        for r in range(replicas)
        for zz in range(NZ)
    ]
    line_in = [
        remote(sq_out.at[2], sq_line.at[i], line_sem, 0, i, z_peer) for i in range(owners * NZ)
    ]

    for q in range(owners):

        @pl.when(rep != first + q)
        def _():
            rs[q].start()

    for k in range(NY):
        slot = NY + k
        for xx in range(NX):
            at = block_at(column(k), xx, 1, 1 - core)
            core_out[slot, xx] = part[pl.ds(at, rows), :].astype(jnp.bfloat16)
        core_copies[slot] = send(core_out.at[slot], core_in.at[slot], core_sem, slot, core_peer)

    def chip_sum(half, k, xx, at):
        start = block_at(column(k), xx, half, core) + at.start
        mine = part[pl.ds(start, at.stop - at.start), :]
        return mine + core_in[half * NY + k, xx, at].astype(jnp.float32)

    x1, y1, x2, y2 = {}, {}, {}, {}

    def x1_slot(half, k, off):
        return (half * NY + k) * (NX - 1) + off - 1

    def y_slot(half, off):
        return half * (NY - 1) + off - 1

    def x_slot(half, off):
        return half * (NX - 1) + off - 1

    def spread(half, k):
        core_copies[half * NY + k].wait_recv()
        for off in far_first(NX)[:-1]:
            slot = x1_slot(half, k, off)
            x1_out[slot] = chip_sum(half, k, lax.rem(x + off, NX), x_part).astype(jnp.bfloat16)
            x1[slot] = send(x1_out.at[slot], x1_in.at[slot], x1_sem, slot, plane_peer(0, off))
        if k != own:
            slot = y_slot(half, offs[k])
            for xx in range(NX):
                y1_out[slot, xx] = chip_sum(half, k, xx, y_part).astype(jnp.bfloat16)
            y1[slot] = send(
                y1_out.at[slot], y1_in.at[slot], y1_sem, slot, plane_peer(offs[k], 0)
            )

    def x_sum(half, k):
        total = chip_sum(half, k, x, x_part)
        for off in range(1, NX):
            slot = x1_slot(half, k, off)
            x1[slot].wait_recv()
            total = total + x1_in[slot].astype(jnp.float32)
        return total

    def y_sum(half, xx):
        total = chip_sum(half, own, xx, y_part)
        for off in range(1, NY):
            total = total + y1_in[y_slot(half, off), xx].astype(jnp.float32)
        return total

    def forward(half):
        for k in range(NY):
            if k != own:
                slot = y_slot(half, offs[k])
                x2_out[slot] = x_sum(half, k).astype(jnp.bfloat16)
                x2[slot] = send(
                    x2_out.at[slot], x2_in.at[slot], x2_sem, slot, plane_peer(offs[k], 0)
                )
        for off in range(1, NY):
            y1[y_slot(half, off)].wait_recv()
        for off in far_first(NX)[:-1]:
            slot = x_slot(half, off)
            y2_out[slot] = y_sum(half, lax.rem(x + off, NX)).astype(jnp.bfloat16)
            y2[slot] = send(y2_out.at[slot], y2_in.at[slot], y2_sem, slot, plane_peer(0, off))

    def gather(half):
        top = x_sum(half, own)
        low = y_sum(half, x)
        for off in range(1, NY):
            slot = y_slot(half, off)
            x2[slot].wait_recv()
            top = top + x2_in[slot].astype(jnp.float32)
        for off in range(1, NX):
            slot = x_slot(half, off)
            y2[slot].wait_recv()
            low = low + y2_in[slot].astype(jnp.float32)
        return top, low

    for k in range(NY):
        spread(0, k)

    @pl.when(owns)
    def _():
        delta_in[rep] = delta[pl.ds(pl.multiple_of(place * shard, 8), shard), :]
        for r in range(replicas):

            @pl.when(rep != r)
            def _():
                rs_in[r].wait_recv()

        total = delta_in[0]
        for r in range(1, replicas):
            total = total + delta_in[r]
        averaged = total / replicas
        avg_ref[pl.ds(pl.multiple_of(place * shard, 8), shard), :] = averaged
        sq_out[0] = jnp.sum(averaged * averaged, axis=0, keepdims=True)
        pair_copy.start()
        for r in range(replicas):

            @pl.when(rep != r)
            def _():
                ag[r].start()

        pair_copy.wait_recv()
        sq_out[1] = sq_out[0] + sq_plane[len(plane)]
        for copy in plane_copies:
            copy.start()

    forward(0)
    for k in range(NY):
        spread(1, k)

    @pl.when(owns)
    def _():
        squares = sq_out[1]
        for i, copy in enumerate(plane_copies):
            copy.wait_recv()
            squares = squares + sq_plane[i]
        sq_out[2] = squares
        sq_line[seat] = squares
        for r in range(replicas):
            for zz in range(NZ):

                @pl.when(other(r, zz))
                def _():
                    line[r * NZ + zz].start()

    z_copy = remote(z_out, z_in, z_sem, 0, 0, z_peer)

    def settle(half):
        top, low = gather(half)

        @pl.when(z == half)
        def _():
            sum_ref[x_part] = top
            sum_ref[y_part] = low

        @pl.when(z != half)
        def _():
            z_out[x_part] = top.astype(jnp.bfloat16)
            z_out[y_part] = low.astype(jnp.bfloat16)
            z_copy.start()

    settle(0)
    forward(1)
    settle(1)
    for q in range(owners):

        @pl.when(rep != first + q)
        def _():
            ag_in[q].wait_recv()

        for zz in range(NZ):

            @pl.when(other(first + q, zz))
            def _():
                line_in[q * NZ + zz].wait_recv()

    squares = sq_line[0]
    for i in range(1, owners * NZ):
        squares = squares + sq_line[i]
    sq_ref[...] = squares

    for copy in sent:
        copy.wait_send()
    for q in range(owners):

        @pl.when(rep != first + q)
        def _():
            rs[q].wait_send()

    @pl.when(owns)
    def _():
        pair_copy.wait_send()
        for copy in plane_copies:
            copy.wait_send()
        for r in range(replicas):

            @pl.when(rep != r)
            def _():
                ag[r].wait_send()

            for zz in range(NZ):

                @pl.when(other(r, zz))
                def _():
                    line[r * NZ + zz].wait_send()

    z_copy.wait_recv()
    sum_ref[...] = sum_ref[...] + z_in[...].astype(jnp.float32)
    z_copy.wait_send()


def exchange(tokens, cotangent, keep_mask, local_params, global_params, order, rows, replicas):
    count, width = tokens.shape
    heads = cotangent.shape[1]
    held, params = global_params.shape
    lines = FRAG * params // LANES
    vmem = pl.BlockSpec(memory_space=pltpu.VMEM)
    hbm = pl.BlockSpec(memory_space=pltpu.HBM)
    bf16, f32 = jnp.bfloat16, jnp.float32
    x_rows = (rows // 16 + 1) // 2 * 16
    x_block, y_block = (x_rows, heads), (rows - x_rows, heads)
    peers = NY * NX - 1
    owners = min(OWNERS, replicas)
    return pl.pallas_call(
        functools.partial(exchange_kernel, replicas),
        out_shape=(
            jax.ShapeDtypeStruct((rows, heads), f32),
            jax.ShapeDtypeStruct((lines, LANES), f32),
            jax.ShapeDtypeStruct((1, LANES), f32),
        ),
        in_specs=[hbm] * 6,
        out_specs=(vmem, vmem, vmem),
        scratch_shapes=[
            pltpu.VMEM((count, width), bf16),
            pltpu.VMEM((count, heads), bf16),
            pltpu.VMEM((1, count), jnp.int32),
            pltpu.VMEM((held, params), f32),
            pltpu.VMEM((held, params), f32),
            pltpu.SMEM(order.shape, jnp.int32),
            pltpu.VMEM((heads, count), bf16),
            pltpu.VMEM((width, heads), f32),
            pltpu.VMEM((2 * NY, NX, rows, heads), bf16),
            pltpu.VMEM((2 * NY, NX, rows, heads), bf16),
            pltpu.VMEM((2 * NY * (NX - 1),) + x_block, bf16),
            pltpu.VMEM((2 * NY * (NX - 1),) + x_block, bf16),
            pltpu.VMEM((2 * (NY - 1), NX) + y_block, bf16),
            pltpu.VMEM((2 * (NY - 1), NX) + y_block, bf16),
            pltpu.VMEM((2 * (NY - 1),) + x_block, bf16),
            pltpu.VMEM((2 * (NY - 1),) + x_block, bf16),
            pltpu.VMEM((2 * (NX - 1),) + y_block, bf16),
            pltpu.VMEM((2 * (NX - 1),) + y_block, bf16),
            pltpu.VMEM((rows, heads), bf16),
            pltpu.VMEM((rows, heads), bf16),
            pltpu.VMEM((lines, LANES), f32),
            pltpu.VMEM((replicas, lines // owners, LANES), f32),
            pltpu.VMEM((3, 1, LANES), f32),
            pltpu.VMEM((peers + 1, 1, LANES), f32),
            pltpu.VMEM((owners * NZ, 1, LANES), f32),
            pltpu.SemaphoreType.DMA((count // TOKEN_BLOCK,)),
            pltpu.SemaphoreType.DMA((5,)),
            pltpu.SemaphoreType.DMA((2, 2 * NY)),
            pltpu.SemaphoreType.DMA((2, 2 * NY * (NX - 1))),
            pltpu.SemaphoreType.DMA((2, 2 * (NY - 1))),
            pltpu.SemaphoreType.DMA((2, 2 * (NY - 1))),
            pltpu.SemaphoreType.DMA((2, 2 * (NX - 1))),
            pltpu.SemaphoreType.DMA((2, 1)),
            pltpu.SemaphoreType.DMA((2, replicas)),
            pltpu.SemaphoreType.DMA((2, replicas)),
            pltpu.SemaphoreType.DMA((2, peers + 1)),
            pltpu.SemaphoreType.DMA((2, replicas * NZ)),
        ],
        compiler_params=pltpu.CompilerParams(
            collective_id=0, has_side_effects=True, vmem_limit_bytes=63 * 1024 * 1024
        ),
        cost_estimate=pl.CostEstimate(
            flops=2 * count * width * heads, bytes_accessed=2 * count * width, transcendentals=0
        ),
    )(tokens, cotangent, keep_mask.reshape(1, count), local_params, global_params, order)


def finish_kernel(
    count,
    order_hbm,
    sum_hbm,
    avg_hbm,
    sq_hbm,
    weight_hbm,
    gain_hbm,
    loc_hbm,
    glob_hbm,
    mom_hbm,
    weight_out,
    gain_out,
    loc_out,
    glob_out,
    mom_out,
    order,
    total,
    avg,
    sq,
    weight,
    gain,
    loc,
    glob,
    mom,
    weight_new,
    gain_new,
    loc_new,
    glob_new,
    mom_new,
    in_sem,
    out_sem,
):
    pairs = [
        (avg_hbm, avg),
        (sq_hbm, sq),
        (loc_hbm.at[0], loc),
        (glob_hbm, glob),
        (mom_hbm, mom),
        (order_hbm, order),
        (sum_hbm, total),
        (weight_hbm.at[0], weight),
        (gain_hbm, gain),
    ]
    loads = [pltpu.make_async_copy(src, dst, in_sem.at[i]) for i, (src, dst) in enumerate(pairs)]
    for copy in loads:
        copy.start()
    for copy in loads:
        copy.wait()

    squares = jnp.sum(sq[...])
    limit = CLIP_RATE * jnp.sqrt(jnp.float32(count))
    factor = jnp.minimum(1.0, limit / jnp.sqrt(jnp.full((8, LANES), squares) + EPSILON))
    held, params = glob.shape
    layer = lax.broadcasted_iota(jnp.int32, (held, LANES), 0)
    first = layer == order[0]
    second = layer == order[1]
    picked = first | second
    lines = params // LANES
    stores = []

    def store(src, dst, index):
        copy = pltpu.make_async_copy(src, dst, out_sem.at[index])
        copy.start()
        stores.append(copy)

    parts = 2
    for part in range(parts):
        for j in range(part * lines // parts, (part + 1) * lines // parts):
            at = slice(j * LANES, (j + 1) * LANES)
            averaged = jnp.where(
                first,
                jnp.broadcast_to(avg[j : j + 1, :], (held, LANES)),
                jnp.broadcast_to(avg[lines + j : lines + j + 1, :], (held, LANES)),
            )
            old_loc, old_glob, old_mom = loc[:, at], glob[:, at], mom[:, at]
            clipped = averaged * factor
            moment_new = MOMENT * old_mom + clipped
            global_new = old_glob - OUTER_RATE * (clipped + MOMENT * moment_new)
            merged = MIX_RATE * old_loc + (1.0 - MIX_RATE) * global_new
            loc_new[:, at] = jnp.where(picked, merged, old_loc)
            glob_new[:, at] = jnp.where(picked, global_new, old_glob)
            mom_new[:, at] = jnp.where(picked, moment_new, old_mom)
        span = pl.ds(part * params // parts, params // parts)
        store(loc_new.at[:, span], loc_out.at[0, :, span], 3 * part)
        store(glob_new.at[:, span], glob_out.at[:, span], 3 * part + 1)
        store(mom_new.at[:, span], mom_out.at[:, span], 3 * part + 2)

    summed = total[...]
    rows, heads = summed.shape
    scale = jnp.broadcast_to(gain[...], (heads, rows)).T
    weight_new[...] = scale * summed
    store(weight_new, weight_out.at[0], 3 * parts)
    product = weight[...].astype(jnp.float32) * summed
    gain_new[...] = jnp.sum(product.T, axis=0, keepdims=True)
    store(gain_new, gain_out, 3 * parts + 1)
    for copy in stores:
        copy.wait()


def finish(order, total, averaged, squares, weight, gain, local_params, global_params, momentum, count):
    hbm = pl.BlockSpec(memory_space=pltpu.HBM)
    f32 = jnp.float32
    shapes = (
        jax.ShapeDtypeStruct(weight.shape, f32),
        jax.ShapeDtypeStruct(gain.shape, f32),
        jax.ShapeDtypeStruct(local_params.shape, f32),
        jax.ShapeDtypeStruct(global_params.shape, f32),
        jax.ShapeDtypeStruct(momentum.shape, f32),
    )
    state = pltpu.VMEM(global_params.shape, f32)
    return pl.pallas_call(
        functools.partial(finish_kernel, count),
        out_shape=shapes,
        in_specs=[hbm] * 9,
        out_specs=(hbm,) * 5,
        scratch_shapes=[
            pltpu.SMEM(order.shape, jnp.int32),
            pltpu.VMEM(total.shape, f32),
            pltpu.VMEM(averaged.shape, f32),
            pltpu.VMEM(squares.shape, f32),
            pltpu.VMEM(weight.shape[1:], weight.dtype),
            pltpu.VMEM(gain.shape, f32),
            state,
            state,
            state,
            pltpu.VMEM(weight.shape[1:], f32),
            pltpu.VMEM(gain.shape, f32),
            state,
            state,
            state,
            pltpu.SemaphoreType.DMA((9,)),
            pltpu.SemaphoreType.DMA((8,)),
        ],
        compiler_params=pltpu.CompilerParams(vmem_limit_bytes=63 * 1024 * 1024),
    )(order, total, averaged, squares, weight, gain, local_params, global_params, momentum)


def per_device(
    replicas,
    fsdp,
    tokens,
    cotangent,
    keep_mask,
    key_weight,
    norm_gain,
    local_params,
    global_params,
    momentum,
    fragment_order,
):
    total, averaged, squares = exchange(
        tokens,
        cotangent,
        keep_mask,
        local_params,
        global_params,
        fragment_order,
        key_weight.shape[1],
        replicas,
    )
    count = FRAG * global_params.shape[1] * fsdp
    return finish(
        fragment_order,
        total,
        averaged,
        squares,
        key_weight,
        norm_gain,
        local_params,
        global_params,
        momentum,
        count,
    )


def solution(mesh):
    in_specs = (
        P(("replica", "fsdp"), None),
        P(("replica", "fsdp"), None),
        P(("replica", "fsdp")),
        P("replica", "fsdp", None),
        P("replica", "fsdp"),
        P("replica", None, "fsdp"),
        P(None, "fsdp"),
        P(None, "fsdp"),
        P(),
    )
    out_specs = (
        P("replica", "fsdp", None),
        P("replica", "fsdp"),
        P("replica", None, "fsdp"),
        P(None, "fsdp"),
        P(None, "fsdp"),
    )
    return jax.shard_map(
        functools.partial(per_device, mesh.shape["replica"], mesh.shape["fsdp"]),
        mesh=mesh,
        in_specs=in_specs,
        out_specs=out_specs,
        check_vma=False,
    )
```
